256 devices in a mesh: lon: 32 (over x_hi, z, core), lat: 8 (over x_lo, y).
Axes of the slice: x: 4 (x_hi: 2, x_lo: 2; x = x_hi * 2 + x_lo), y: 4, z: 8, core: 2. Of those that a mesh axis runs over, the one named last changes fastest.
Arguments:
- node_latents: bfloat16 [8192, 512], P(('lon', 'lat')), may hold values from -24 to 24
- edge_latents: bfloat16 [65536, 512], P(('lon', 'lat')), may hold values from -24 to 24
- coarse_edges: bfloat16 [2048, 512], P(('lon', 'lat')), may hold values from -6 to 6
- sender: int32 [65536], P(('lon', 'lat')), may hold values from 0 to 63, as said below
- receiver: int32 [65536], P(('lon', 'lat')), may hold values from 0 to 31
- halo_send: int32 [256, 4, 8], P(('lon', 'lat')), may hold values from 0 to 31
- coarse_row: int32 [512], P(('lon', 'lat')), may hold values from 0 to 31
- coarse_sender: int32 [2048], P(('lon', 'lat')), may hold values from 0 to 511
- coarse_receiver: int32 [2048], P(('lon', 'lat')), may hold values from 0 to 511
- edge_mixer: bfloat16 [3, 512, 512], replicated, may hold values from -0.15625 to 0.15625
- edge_output: bfloat16 [512, 512], replicated, may hold values from -0.25 to 0.25
- node_mixer: bfloat16 [2, 512, 512], replicated, may hold values from -0.1875 to 0.1875
- node_output: bfloat16 [512, 512], replicated, may hold values from -0.25 to 0.25
- node_cotangent: bfloat16 [8192, 512], P(('lon', 'lat')), may hold values from -6 to 6
- edge_cotangent: bfloat16 [65536, 512], P(('lon', 'lat')), may hold values from -6 to 6
- coarse_cotangent: bfloat16 [2048, 512], P(('lon', 'lat')), may hold values from -6 to 6
Outputs:
- node_update: bfloat16 [8192, 512], P(('lon', 'lat'))
- edge_update: bfloat16 [65536, 512], P(('lon', 'lat'))
- coarse_update: bfloat16 [2048, 512], P(('lon', 'lat'))
- node_grad: bfloat16 [8192, 512], P(('lon', 'lat'))
- edge_grad: bfloat16 [65536, 512], P(('lon', 'lat'))
- coarse_grad: bfloat16 [2048, 512], P(('lon', 'lat'))
- edge_mixer_grad: float32 [3, 262144], P(None, ('lon', 'lat'))
- edge_output_grad: float32 [262144], P(('lon', 'lat'))
- node_mixer_grad: float32 [2, 262144], P(None, ('lon', 'lat'))
- node_output_grad: float32 [262144], P(('lon', 'lat'))
The draws below stay inside these ranges and needn't reach their ends.
Inputs may be any that keep to these rules, and one draw needn't show every extreme that they name: `sender`: A value below 32 is a row of the edge's own device; 32 + k * 8 + h names row h of what arrives from neighbour k (0 lower lon, 1 upper lon, 2 lower lat, 3 upper lat); a device at an end of lat never names the missing lat neighbour.
All inputs are finite; a program needn't handle non-finite values.
Results may differ from the reference program's by a relative error of at most 0.012.
Values may be sent and summed in bfloat16 or wider, within the bound.
No kernel may reach another device: no remote copies, remote signals or barrier semaphores. Data moves between devices by JAX's collectives and lax.ppermute only.
A program may use at most 128 MiB of HBM per device.

```python
import jax
import jax.numpy as jnp
from jax import lax

D = 512
NODE_DEV = 32
HALO = 8
EDGE_DEV = 256
COARSE_DEV = 2
NODES = 8192
EDGES = 65536
COARSE = 512
CEDGES = 2048
N_LON = 32
N_LAT = 8


def draw_sender(key, part):
    key = jax.random.fold_in(key, 7)
    first, second, third = jax.random.split(key, 3)
    kind = jax.random.randint(first, (EDGES,), 0, 8)
    local = jax.random.randint(second, (EDGES,), 0, NODE_DEV)
    place = jax.random.randint(third, (EDGES,), 0, HALO)
    device = jnp.arange(EDGES) // EDGE_DEV
    band = device % N_LAT
    missing = (kind == 6) & (band == 0) | (kind == 7) & (band == N_LAT - 1)
    rim_index = jnp.where(kind >= 4, kind - 4, 0)
    value = jnp.where((kind < 4) | missing, local, NODE_DEV + rim_index * HALO + place)
    return value.astype(jnp.int32)


def with_ends(result, rng, least, high):
    longest = result.shape.index(max(result.shape))
    spots = []
    for shift in (0, 1):
        where = [jax.random.randint(jax.random.fold_in(rng, axis), (), 0, length) for axis, length in enumerate(result.shape)]
        where[longest] = (where[longest] + shift) % result.shape[longest]
        spots.append(tuple(where))
    return result.at[spots[0]].set(least).at[spots[1]].set(high)


def raised(values, own_key, source, target, blocks, factor):
    owner, partner = [(jnp.arange(values.shape[position]) // (values.shape[position] // blocks)).reshape([-1 if axis == position else 1 for axis in range(values.ndim)]) for position in (source, target)]
    chosen = jax.random.permutation(own_key, blocks)[partner]
    strong = (owner == chosen) | (owner == (partner + blocks // 2) % blocks)
    return jnp.where(strong, factor * values, values)


def level_of(key, dims, pieces, least, high):
    factor_of = 1.0
    for position, shards_of in pieces:
        heights = jax.random.uniform(jax.random.fold_in(jax.random.fold_in(key, 6), position), (shards_of,), jnp.float32, least / len(pieces), high / len(pieces))
        factor_of = factor_of * jnp.repeat(jnp.exp(heights), dims[position] // shards_of).reshape((-1,) + (1,) * (len(dims) - 1 - position))
    return factor_of


def scatter_about(stream_key, extent, scale, bound, pieces=(), held_as=jnp.bfloat16):
    result = jax.random.normal(stream_key, extent, jnp.float32) * scale
    if len(pieces) > 0:
        result = level_of(stream_key, extent, pieces, -0.22, 0.18) * result
    return jnp.clip(result, min=-bound, max=bound).astype(held_as)


def heavy_noise(stream_key, shape, width, reach, shards, heavy, held_as=jnp.bfloat16):
    drawn = width * jax.random.normal(stream_key, shape, jnp.float32)
    if shards:
        drawn = drawn * level_of(stream_key, shape, shards, -0.22, 0.18)
    return jnp.clip(raised(drawn, jax.random.fold_in(stream_key, 3), *heavy), -reach, reach).astype(held_as)


def setup_inputs(seed: int = 0) -> dict:
    keys = jax.random.split(jax.random.key(seed), 17)
    return {
        "node_latents": heavy_noise(keys[0], (NODES, D), 1.0, 24.0, ((0, 256),), (0, 1, 256, 6.0)),
        "edge_latents": heavy_noise(keys[1], (EDGES, D), 1.0, 24.0, ((0, 256),), (0, 1, 256, 6.0)),
        "coarse_edges": scatter_about(keys[2], (CEDGES, D), 1.0, 6.0, ((0, 256),)),
        "sender": draw_sender(jax.random.fold_in(keys[16], 71), 0),
        "receiver": with_ends(jax.random.randint(keys[4], (EDGES,), 0, NODE_DEV), jax.random.fold_in(keys[4], 1), 0, NODE_DEV - 1).astype(jnp.int32),
        "halo_send": with_ends(jax.random.randint(keys[5], (N_LON * N_LAT, 4, HALO), 0, NODE_DEV), jax.random.fold_in(keys[5], 1), 0, NODE_DEV - 1).astype(jnp.int32),
        "coarse_row": with_ends(jax.random.randint(keys[6], (COARSE,), 0, NODE_DEV), jax.random.fold_in(keys[6], 1), 0, NODE_DEV - 1).astype(jnp.int32),
        "coarse_sender": with_ends(jax.random.randint(keys[7], (CEDGES,), 0, COARSE), jax.random.fold_in(keys[7], 1), 0, COARSE - 1).astype(jnp.int32),
        "coarse_receiver": with_ends(jax.random.randint(keys[8], (CEDGES,), 0, COARSE), jax.random.fold_in(keys[8], 1), 0, COARSE - 1).astype(jnp.int32),
        "edge_mixer": scatter_about(keys[9], (3, D, D), (3 * D) ** -0.5, 0.15625),
        "edge_output": scatter_about(keys[10], (D, D), D ** -0.5, 0.25),
        "node_mixer": scatter_about(keys[11], (2, D, D), (2 * D) ** -0.5, 0.1875),
        "node_output": scatter_about(keys[12], (D, D), D ** -0.5, 0.25),
        "node_cotangent": scatter_about(keys[13], (NODES, D), 1.0, 6.0, ((0, 256),)),
        "edge_cotangent": scatter_about(keys[14], (EDGES, D), 1.0, 6.0, ((0, 256),)),
        "coarse_cotangent": scatter_about(keys[15], (CEDGES, D), 1.0, 6.0, ((0, 256),)),
    }


epsilon = 1e-05

def matmul(left, right):
    return jnp.dot(left, right, preferred_element_type=jnp.float32)

def outer_sum(left, right):
    return jnp.dot(left.T, right, preferred_element_type=jnp.float32)

def normalize(values):
    center = values - lax.optimization_barrier(jnp.mean(values, -1, keepdims=True))
    spread = lax.optimization_barrier(jnp.mean(center * center, -1, keepdims=True))
    scale_r = lax.rsqrt(spread + epsilon)
    return (center * scale_r, scale_r)

def normalize_back(normed, scale_r, incoming):
    mean_g = lax.optimization_barrier(jnp.mean(incoming, -1, keepdims=True))
    mean_gy = lax.optimization_barrier(jnp.mean(incoming * normed, -1, keepdims=True))
    return scale_r * (incoming - mean_g - normed * mean_gy)

def swish_slope(values):
    sigma = jax.nn.sigmoid(values)
    return sigma * (1.0 + values * (1.0 - sigma))

def edge_forward(send_rows, recv_rows, edge_rows, edge_mixer, edge_output):
    pre_act = matmul(send_rows, edge_mixer[0]) + matmul(recv_rows, edge_mixer[1]) + matmul(edge_rows, edge_mixer[2])
    edge_hidden = jax.nn.silu(pre_act).astype(jnp.bfloat16)
    normed, scale_r = normalize(matmul(edge_hidden, edge_output))
    message = normed.astype(jnp.bfloat16)
    updated = (edge_rows.astype(jnp.float32) + message.astype(jnp.float32)).astype(jnp.bfloat16)
    return (pre_act, edge_hidden, normed, scale_r, message, updated)

def edge_backward(pre_act, edge_hidden, normed, scale_r, grad_message, send_rows, recv_rows, edge_rows, edge_cot, edge_mixer, edge_output):
    grad_pre = normalize_back(normed, scale_r, grad_message).astype(jnp.bfloat16)
    grad_act = (matmul(grad_pre, edge_output.T) * swish_slope(pre_act)).astype(jnp.bfloat16)
    weight_terms = (outer_sum(send_rows, grad_act), outer_sum(recv_rows, grad_act), outer_sum(edge_rows, grad_act), outer_sum(edge_hidden, grad_pre))
    grad_send = matmul(grad_act, edge_mixer[0].T)
    grad_recv = matmul(grad_act, edge_mixer[1].T)
    grad_rows = (edge_cot.astype(jnp.float32) + matmul(grad_act, edge_mixer[2].T)).astype(jnp.bfloat16)
    return (weight_terms, grad_send, grad_recv, grad_rows)

def reference(node_latents, edge_latents, coarse_edges, sender, receiver, halo_send, coarse_row, coarse_sender, coarse_receiver, edge_mixer, edge_output, node_mixer, node_output, node_cotangent, edge_cotangent, coarse_cotangent):
    edge_device = (jnp.arange(EDGES) // EDGE_DEV).astype(jnp.int32)
    edge_lon = edge_device // N_LAT
    edge_lat = edge_device % N_LAT
    rim_slot = sender - NODE_DEV
    rim_index = jnp.clip(rim_slot // HALO, 0, 3)
    rim_place = rim_slot % HALO
    source_lon = jnp.where(rim_index == 0, (edge_lon - 1) % N_LON, jnp.where(rim_index == 1, (edge_lon + 1) % N_LON, edge_lon))
    source_lat = jnp.where(rim_index == 2, edge_lat - 1, jnp.where(rim_index == 3, edge_lat + 1, edge_lat))
    source_lat = jnp.clip(source_lat, 0, N_LAT - 1)
    source_device = source_lon * N_LAT + source_lat
    list_index = rim_index + 1 - 2 * (rim_index % 2)
    remote_row = halo_send[source_device, list_index, rim_place]
    send_global = jnp.where(sender < NODE_DEV, edge_device * NODE_DEV + sender, source_device * NODE_DEV + remote_row).astype(jnp.int32)
    recv_global = (edge_device * NODE_DEV + receiver).astype(jnp.int32)
    member_rows = (jnp.arange(COARSE) // COARSE_DEV * NODE_DEV + coarse_row).astype(jnp.int32)
    coarse_send = member_rows[coarse_sender]
    coarse_recv = member_rows[coarse_receiver]
    send_rows = jnp.concatenate([node_latents[send_global], node_latents[coarse_send]], 0)
    recv_rows = jnp.concatenate([node_latents[recv_global], node_latents[coarse_recv]], 0)
    edge_rows = jnp.concatenate([edge_latents, coarse_edges], 0)
    pre_act, edge_hidden, normed, scale_r, message, updated = edge_forward(send_rows, recv_rows, edge_rows, edge_mixer, edge_output)
    message_wide = message.astype(jnp.float32)
    coarse_sum = jax.ops.segment_sum(message_wide[EDGES:], coarse_receiver, num_segments=COARSE)
    aggregate = jax.ops.segment_sum(message_wide[:EDGES], recv_global, num_segments=NODES)
    aggregate = aggregate + jax.ops.segment_sum(coarse_sum, member_rows, num_segments=NODES)
    agg_round = aggregate.astype(jnp.bfloat16)
    node_pre = matmul(node_latents, node_mixer[0]) + matmul(agg_round, node_mixer[1])
    node_hidden = jax.nn.silu(node_pre).astype(jnp.bfloat16)
    node_normed, node_scale = normalize(matmul(node_hidden, node_output))
    node_update = (node_latents.astype(jnp.float32) + node_normed).astype(jnp.bfloat16)
    grad_update = normalize_back(node_normed, node_scale, node_cotangent.astype(jnp.float32)).astype(jnp.bfloat16)
    node_output_grad = outer_sum(node_hidden, grad_update).reshape(-1)
    grad_node_pre = (matmul(grad_update, node_output.T) * swish_slope(node_pre)).astype(jnp.bfloat16)
    node_mixer_grad = jnp.stack([outer_sum(node_latents, grad_node_pre), outer_sum(agg_round, grad_node_pre)]).reshape(2, -1)
    grad_aggregate = matmul(grad_node_pre, node_mixer[1].T).astype(jnp.bfloat16)
    grad_message = jnp.concatenate([grad_aggregate[recv_global], grad_aggregate[coarse_recv]], 0).astype(jnp.float32)
    grad_message = grad_message + jnp.concatenate([edge_cotangent, coarse_cotangent], 0).astype(jnp.float32)
    edge_cot = jnp.concatenate([edge_cotangent, coarse_cotangent], 0)
    weight_terms, grad_send, grad_recv, grad_rows = edge_backward(pre_act, edge_hidden, normed, scale_r, grad_message, send_rows, recv_rows, edge_rows, edge_cot, edge_mixer, edge_output)
    node_total = node_cotangent.astype(jnp.float32) + matmul(grad_node_pre, node_mixer[0].T)
    node_total = node_total + jax.ops.segment_sum(grad_send[:EDGES], send_global, num_segments=NODES)
    node_total = node_total + jax.ops.segment_sum(grad_recv[:EDGES], recv_global, num_segments=NODES)
    coarse_total = jax.ops.segment_sum(grad_send[EDGES:], coarse_sender, num_segments=COARSE)
    coarse_total = coarse_total + jax.ops.segment_sum(grad_recv[EDGES:], coarse_receiver, num_segments=COARSE)
    node_total = node_total + jax.ops.segment_sum(coarse_total, member_rows, num_segments=NODES)
    edge_mixer_grad = jnp.stack(list(weight_terms[:3])).reshape(3, -1)
    edge_output_grad = weight_terms[3].reshape(-1)
    return (node_update, updated[:EDGES], updated[EDGES:], node_total.astype(jnp.bfloat16), grad_rows[:EDGES], grad_rows[EDGES:], edge_mixer_grad, edge_output_grad, node_mixer_grad, node_output_grad)
```

```python
import jax
import jax.numpy as jnp
import numpy as np
from jax import lax
from jax.experimental import pallas as pl
from jax.experimental.pallas import tpu as pltpu
from jax.sharding import Mesh
from jax.sharding import PartitionSpec as P

epsilon = 1e-05
bf16 = jnp.bfloat16
f32 = jnp.float32

ALL = ("xhi", "z", "core", "xlo", "y")
SHAPE = (2, 8, 2, 2, 4)
LON = ("xhi", "z", "core")
LAT = ("xlo", "y")
CHIPS = ("xhi", "z", "xlo", "y")
PLANE = ("xhi", "xlo", "y")
D = 512
NODE = 32
EDGE = 256
CEDGE = 8
RIM = 8
ROWS = EDGE + 16
TABLE = NODE + 4 * RIM


def dot(left, right):
    return lax.dot_general(left, right, (((1,), (0,)), ((), ())), preferred_element_type=f32)


def dot_nt(left, right):
    return lax.dot_general(left, right, (((1,), (1,)), ((), ())), preferred_element_type=f32)


def dot_tn(left, right):
    return lax.dot_general(left, right, (((0,), (0,)), ((), ())), preferred_element_type=f32)


def sigmoid(v):
    return 1.0 / (1.0 + jnp.exp(-v))


def normalize(values):
    center = values - jnp.mean(values, -1, keepdims=True)
    spread = jnp.mean(center * center, -1, keepdims=True)
    scale_r = lax.rsqrt(spread + epsilon)
    return (center * scale_r, scale_r)


def normalize_back(normed, scale_r, incoming):
    mean_g = jnp.mean(incoming, -1, keepdims=True)
    mean_gy = jnp.mean(incoming * normed, -1, keepdims=True)
    return scale_r * (incoming - mean_g - normed * mean_gy)


def swish_slope(values):
    sigma = sigmoid(values)
    return sigma * (1.0 + values * (1.0 - sigma))


def pick_t(count, targets):
    shape = (count, targets.shape[1])
    hit = lax.broadcasted_iota(jnp.int32, shape, 0) == targets
    return jnp.where(hit, 1.0, 0.0).astype(bf16)


def order_matrix(core):
    wide = (D, 128)
    p = lax.broadcasted_iota(jnp.int32, wide, 0)
    half = p >> 8
    plane = (p >> 4) & 15
    depth = (p >> 1) & 7
    side = lax.bitwise_xor(half, core)
    f = ((plane >> 3) << 8) + (depth << 5) + (side << 4) + ((plane & 7) << 1) + (p & 1)
    lane = lax.broadcasted_iota(jnp.int32, wide, 1)
    parts = [jnp.where(f == lane + 128 * j, 1.0, 0.0).astype(bf16) for j in range(D // 128)]
    return jnp.concatenate(parts, axis=1)


def fold(row):
    return jnp.concatenate([row[:, 128 * j : 128 * (j + 1)] for j in range(4)], axis=0)


def unfold(block):
    return jnp.concatenate([block[j : j + 1, :] for j in range(4)], axis=1)


def chip_of(c):
    return (c >> 5) * 8 + ((c >> 1) & 7)


def side_of(c):
    return (c >> 4) & 1


def coarse_pick(same_ref, other_ref, core, c):
    chip = chip_of(c)
    here = (side_of(c) == core).astype(f32)
    block = same_ref[chip].astype(f32) * here + other_ref[chip].astype(f32) * (1.0 - here)
    low = ((c & 1) == 0).astype(f32)
    return unfold(block[0:4] * low + block[4:8] * (1.0 - low))


def start_kernel(core_row_ref, halo_ref, nodes_ref, h0, h1, h2, h3, spread_ref, table, picked):
    table[...] = nodes_ref[...].astype(f32)
    for k, out in enumerate((h0, h1, h2, h3)):
        for h in range(RIM):
            picked[h : h + 1, :] = table[pl.ds(halo_ref[0, k, h], 1), :]
        out[...] = picked[...].astype(bf16)
    rows = [fold(table[pl.ds(core_row_ref[r], 1), :]) for r in range(2)]
    block = jnp.concatenate(rows, axis=0).astype(bf16)
    spread_ref[...] = jnp.broadcast_to(block[None], spread_ref.shape)


def forward_kernel(
    core_ref,
    csend_ref,
    crecv_ref,
    nodes_ref,
    h0,
    h1,
    h2,
    h3,
    same_ref,
    other_ref,
    edges_ref,
    cedges_ref,
    sender_ref,
    receiver_ref,
    mixer_ref,
    output_ref,
    update_ref,
    cupdate_ref,
    pre_ref,
    hidden_ref,
    normed_ref,
    scale_ref,
    send_ref,
    recv_ref,
    agg_ref,
    cmsg_ref,
):
    core = core_ref[0]
    nodes = nodes_ref[...]
    rims = [h[...].astype(f32) for h in (h0, h1, h2, h3)]
    table = jnp.concatenate([nodes.astype(f32)] + rims, axis=0).astype(bf16)
    from_t = pick_t(TABLE, sender_ref[...])
    into_t = pick_t(NODE, receiver_ref[...])
    blank = jnp.zeros((16 - CEDGE, D), f32)
    csend = [coarse_pick(same_ref, other_ref, core, csend_ref[e]) for e in range(CEDGE)]
    crecv = [coarse_pick(same_ref, other_ref, core, crecv_ref[e]) for e in range(CEDGE)]
    send_ref[0:EDGE, :] = dot_tn(from_t, table).astype(bf16)
    send_ref[EDGE:ROWS, :] = jnp.concatenate(csend + [blank], axis=0).astype(bf16)
    recv_ref[0:EDGE, :] = dot_tn(into_t, nodes).astype(bf16)
    recv_ref[EDGE:ROWS, :] = jnp.concatenate(crecv + [blank], axis=0).astype(bf16)
    cedges = cedges_ref[...].astype(f32)
    tail = jnp.concatenate([cedges, blank], axis=0).astype(bf16)
    edges = edges_ref[...]
    rows = jnp.concatenate([edges, tail], axis=0)
    pre = dot(send_ref[...], mixer_ref[0]) + dot(recv_ref[...], mixer_ref[1]) + dot(rows, mixer_ref[2])
    pre_ref[...] = pre
    hidden = (pre * sigmoid(pre)).astype(bf16)
    hidden_ref[...] = hidden
    normed, scale_r = normalize(dot(hidden, output_ref[...]))
    normed_ref[...] = normed
    scale_ref[...] = jnp.broadcast_to(scale_r, scale_ref.shape)
    message = normed.astype(bf16)
    wide = message.astype(f32)
    update_ref[...] = (edges.astype(f32) + wide[0:EDGE]).astype(bf16)
    cupdate_ref[...] = (cedges + wide[EDGE : EDGE + CEDGE]).astype(bf16)
    agg_ref[...] = dot(into_t, message[0:EDGE])
    cmsg_ref[...] = wide[EDGE : EDGE + CEDGE].astype(bf16)


def spread_kernel(core_ref, mine_ref, theirs_ref, msg_ref, sib_ref, out_ref, total):
    core = core_ref[0]
    total[...] = jnp.zeros_like(total)
    for index_ref, rows_ref in ((mine_ref, msg_ref), (theirs_ref, sib_ref)):
        rows = rows_ref[...].astype(f32)
        for e in range(CEDGE):
            c = index_ref[e]
            here = (side_of(c) == core).astype(f32)
            low = ((c & 1) == 0).astype(f32)
            piece = fold(rows[e : e + 1, :])
            chip = chip_of(c)
            block = jnp.concatenate([piece * (here * low), piece * (here * (1.0 - low))], axis=0)
            total[chip] = total[chip] + block
    out_ref[...] = total[...].astype(bf16)


def put_halves(keep_ref, give_ref, slot, grad):
    keep_ref[:, slot] = grad[0 : D // 2].astype(bf16).reshape(16, 16, D)
    give_ref[:, slot] = grad[D // 2 : D].astype(bf16).reshape(16, 16, D)


def node_kernel(
    core_ref,
    coarse_row_ref,
    sums_ref,
    agg_ref,
    nodes_ref,
    mixer_ref,
    output_ref,
    cot_ref,
    update_ref,
    base_ref,
    grad_agg_ref,
    spread_ref,
    keep_ref,
    give_ref,
):
    owned = jnp.sum(sums_ref[...].astype(f32), axis=0)
    place = lax.broadcasted_iota(jnp.int32, (NODE, D), 0)
    aggregate = agg_ref[...]
    for r in range(2):
        row = unfold(owned[4 * r : 4 * r + 4])
        aggregate = aggregate + jnp.where(place == coarse_row_ref[r], row, 0.0)
    rounded = aggregate.astype(bf16)
    nodes = nodes_ref[...]
    cot = cot_ref[...].astype(f32)
    pre = dot(nodes, mixer_ref[0]) + dot(rounded, mixer_ref[1])
    hidden = (pre * sigmoid(pre)).astype(bf16)
    normed, scale_r = normalize(dot(hidden, output_ref[...]))
    update_ref[...] = (nodes.astype(f32) + normed).astype(bf16)
    grad_update = normalize_back(normed, scale_r, cot).astype(bf16)
    grad_pre = (dot_nt(grad_update, output_ref[...]) * swish_slope(pre)).astype(bf16)
    grad_agg = dot_nt(grad_pre, mixer_ref[1]).astype(bf16)
    grad_agg_ref[...] = grad_agg
    wide = grad_agg.astype(f32)
    rows = []
    for r in range(2):
        row = jnp.sum(jnp.where(place == coarse_row_ref[r], wide, 0.0), axis=0, keepdims=True)
        rows.append(fold(row))
    block = jnp.concatenate(rows, axis=0).astype(bf16)
    spread_ref[...] = jnp.broadcast_to(block[None], spread_ref.shape)
    base_ref[...] = cot + dot_nt(grad_pre, mixer_ref[0])
    order = order_matrix(core_ref[0])
    for slot, (left, right) in enumerate(((nodes, grad_pre), (rounded, grad_pre), (hidden, grad_update))):
        put_halves(keep_ref, give_ref, slot, dot(dot_nt(order, left).astype(bf16), right))


def backward_kernel(
    core_ref,
    csend_ref,
    crecv_ref,
    same_ref,
    other_ref,
    grad_agg_ref,
    sender_ref,
    receiver_ref,
    edges_ref,
    cedges_ref,
    ecot_ref,
    ccot_ref,
    pre_ref,
    hidden_ref,
    normed_ref,
    scale_ref,
    send_ref,
    recv_ref,
    mixer_ref,
    output_ref,
    grad_ref,
    cgrad_ref,
    local_ref,
    g0,
    g1,
    g2,
    g3,
    keep_ref,
    give_ref,
    spread,
):
    core = core_ref[0]
    into_t = pick_t(NODE, receiver_ref[...])
    from_t = pick_t(TABLE, sender_ref[...])
    blank = jnp.zeros((16 - CEDGE, D), f32)
    ecot = ecot_ref[...].astype(f32)
    ccot = ccot_ref[...].astype(f32)
    cgrads = [coarse_pick(same_ref, other_ref, core, crecv_ref[e]) for e in range(CEDGE)]
    fine = dot_tn(into_t, grad_agg_ref[...]) + ecot
    coarse = jnp.concatenate(cgrads, axis=0) + ccot
    incoming = jnp.concatenate([fine, coarse, blank], axis=0)
    scale_r = scale_ref[:, 0:1]
    grad_pre = normalize_back(normed_ref[...], scale_r, incoming).astype(bf16)
    grad_act = (dot_nt(grad_pre, output_ref[...]) * swish_slope(pre_ref[...])).astype(bf16)

    order = order_matrix(core)
    tail = jnp.concatenate([cedges_ref[...].astype(f32), blank], axis=0).astype(bf16)
    rows = jnp.concatenate([edges_ref[...], tail], axis=0)
    for slot, (left, right) in enumerate(
        ((send_ref[...], grad_act), (recv_ref[...], grad_act), (rows, grad_act), (hidden_ref[...], grad_pre))
    ):
        put_halves(keep_ref, give_ref, slot, dot(dot_nt(order, left).astype(bf16), right))

    grad_rows = dot_nt(grad_act, mixer_ref[2])
    grad_ref[...] = (ecot + grad_rows[0:EDGE]).astype(bf16)
    cgrad_ref[...] = (ccot + grad_rows[EDGE : EDGE + CEDGE]).astype(bf16)
    fine_act = grad_act[0:EDGE]
    coarse_act = grad_act[EDGE:ROWS]
    by_sender = jnp.concatenate([dot(from_t, fine_act).astype(bf16), coarse_act], axis=0)
    by_receiver = jnp.concatenate([dot(into_t, fine_act).astype(bf16), coarse_act], axis=0)
    to_sender = dot_nt(by_sender, mixer_ref[0])
    to_receiver = dot_nt(by_receiver, mixer_ref[1])
    local_ref[...] = to_sender[0:NODE] + to_receiver[0:NODE]
    for k, out in enumerate((g0, g1, g2, g3)):
        out[...] = to_sender[NODE + RIM * k : NODE + RIM * (k + 1)].astype(bf16)

    spread[...] = jnp.zeros_like(spread)
    for index_ref, grads in ((csend_ref, to_sender[TABLE:]), (crecv_ref, to_receiver[NODE:])):
        for e in range(CEDGE):
            c = index_ref[e]
            half = lax.bitwise_xor(side_of(c), core)
            plane = (c >> 8) * 8 + ((c >> 1) & 7)
            at = pl.ds(((c >> 5) & 7) * 2 + (c & 1), 1)
            spread[half, plane, at, :] = spread[half, plane, at, :] + grads[e : e + 1, :]
    keep_ref[:, 4] = spread[0].astype(bf16)
    give_ref[:, 4] = spread[1].astype(bf16)


def chip_sum_kernel(keep_e, got_e, keep_n, got_n, out_ref):
    for d in range(16):
        out_ref[d, 0:5] = (keep_e[d].astype(f32) + got_e[d].astype(f32)).astype(bf16)
        out_ref[d, 5:8] = (keep_n[d].astype(f32) + got_n[d].astype(f32)).astype(bf16)


def plane_sum_kernel(in_ref, out_ref):
    total = in_ref[0].astype(f32)
    for d in range(1, 16):
        total = total + in_ref[d].astype(f32)
    total = total.reshape(128, D).astype(bf16)
    place = lax.broadcasted_iota(jnp.int32, (128, 128), 0)
    source = ((place >> 1) & 7) * 16 + (place >> 4) * 2 + (place & 1)
    hit = source == lax.broadcasted_iota(jnp.int32, (128, 128), 1)
    ordered = dot(jnp.where(hit, 1.0, 0.0).astype(bf16), total).astype(bf16)
    out_ref[...] = ordered.reshape(8, 16, D)


def finish_kernel(
    coarse_row_ref,
    halo_ref,
    sums_ref,
    base_ref,
    local_ref,
    r0,
    r1,
    r2,
    r3,
    node_grad_ref,
    mix_ref,
    out_ref,
    node_mix_ref,
    node_out_ref,
    total,
    back,
):
    owned = jnp.sum(sums_ref[...].astype(f32), axis=0)
    total[...] = base_ref[...] + local_ref[...]
    for k, got in enumerate((r0, r1, r2, r3)):
        back[...] = got[...].astype(f32)
        for h in range(RIM):
            at = pl.ds(halo_ref[0, k, h], 1)
            total[at, :] = total[at, :] + back[h : h + 1, :]
    for r in range(2):
        at = pl.ds(coarse_row_ref[r], 1)
        total[at, :] = total[at, :] + owned[8 + r : 9 + r]
        wide = slice(D * r, D * (r + 1))
        for a in range(3):
            mix_ref[a : a + 1, wide] = owned[2 * a + r : 2 * a + r + 1]
        out_ref[:, wide] = owned[6 + r : 7 + r]
        for a in range(2):
            node_mix_ref[a : a + 1, wide] = owned[10 + 2 * a + r : 11 + 2 * a + r]
        node_out_ref[:, wide] = owned[14 + r : 15 + r]
    node_grad_ref[...] = total[...].astype(bf16)


def call(kernel, outs, scalars, arrays, scratch=(), flops=0):
    smem = pl.BlockSpec(memory_space=pltpu.SMEM)
    vmem = pl.BlockSpec(memory_space=pltpu.VMEM)
    moved = sum(int(np.prod(a.shape)) * a.dtype.itemsize for a in arrays)
    moved += sum(int(np.prod(o.shape)) * o.dtype.itemsize for o in outs)
    return pl.pallas_call(
        kernel,
        out_shape=outs,
        in_specs=[smem] * len(scalars) + [vmem] * len(arrays),
        out_specs=[vmem] * len(outs),
        scratch_shapes=list(scratch),
        compiler_params=pltpu.CompilerParams(vmem_limit_bytes=40 * 2**20),
        cost_estimate=pl.CostEstimate(flops=flops, bytes_accessed=moved, transcendentals=0),
    )(*scalars, *arrays)


def shaped(shape, dtype):
    return jax.ShapeDtypeStruct(shape, dtype)


def swap(x):
    return lax.ppermute(x, "core", [(0, 1), (1, 0)])


def up(x, axes, count, closed):
    ends = count if closed else count - 1
    return lax.ppermute(x, axes, [(i, (i + 1) % count) for i in range(ends)])


def down(x, axes, count, closed):
    ends = count if closed else count - 1
    return lax.ppermute(x, axes, [((i + 1) % count, i) for i in range(ends)])


def to_neighbours(a0, a1, a2, a3):
    return (
        up(a1, LON, 32, True),
        down(a0, LON, 32, True),
        up(a3, LAT, 8, False),
        down(a2, LAT, 8, False),
    )


def swapped_blocks(x, axes):
    return lax.all_to_all(x, axes, 0, 0, tiled=True)


def shards(
    node_latents,
    edge_latents,
    coarse_edges,
    sender,
    receiver,
    halo_send,
    coarse_row,
    coarse_sender,
    coarse_receiver,
    edge_mixer,
    edge_output,
    node_mixer,
    node_output,
    node_cotangent,
    edge_cotangent,
    coarse_cotangent,
):
    core = lax.axis_index("core").astype(jnp.int32).reshape(1)
    sender = sender.reshape(1, EDGE)
    receiver = receiver.reshape(1, EDGE)
    sib_receiver = swap(coarse_receiver)
    rim = shaped((RIM, D), bf16)
    blocks = shaped((128, 8, 128), bf16)

    *rims, spread = call(
        start_kernel,
        [rim] * 4 + [blocks],
        (coarse_row, halo_send),
        (node_latents,),
        [pltpu.VMEM((NODE, D), f32), pltpu.VMEM((RIM, D), f32)],
    )
    rims = to_neighbours(*rims)
    same = swapped_blocks(spread, CHIPS)
    other = swap(same)

    wide = shaped((ROWS, D), f32)
    half = shaped((ROWS, D), bf16)
    update, cupdate, pre, hidden, normed, scale_r, send_rows, recv_rows, agg, cmsg = call(
        forward_kernel,
        [
            shaped((EDGE, D), bf16),
            shaped((CEDGE, D), bf16),
            wide,
            half,
            wide,
            shaped((ROWS, 128), f32),
            half,
            half,
            shaped((NODE, D), f32),
            shaped((CEDGE, D), bf16),
        ],
        (core, coarse_sender, coarse_receiver),
        (
            node_latents,
            *rims,
            same,
            other,
            edge_latents,
            coarse_edges,
            sender,
            receiver,
            edge_mixer,
            edge_output,
        ),
    )
    (sums,) = call(
        spread_kernel,
        [blocks],
        (core, coarse_receiver, sib_receiver),
        (cmsg, swap(cmsg)),
        [pltpu.VMEM((128, 8, 128), f32)],
    )
    sums = swapped_blocks(sums, CHIPS)

    node_update, base, grad_agg, spread, keep_n, give_n = call(
        node_kernel,
        [
            shaped((NODE, D), bf16),
            shaped((NODE, D), f32),
            shaped((NODE, D), bf16),
            blocks,
            shaped((16, 3, 16, D), bf16),
            shaped((16, 3, 16, D), bf16),
        ],
        (core, coarse_row),
        (sums, agg, node_latents, node_mixer, node_output, node_cotangent),
    )
    got_n = swap(give_n)
    same = swapped_blocks(spread, CHIPS)
    other = swap(same)

    grad, cgrad, local, *backs, keep_e, give_e = call(
        backward_kernel,
        [shaped((EDGE, D), bf16), shaped((CEDGE, D), bf16), shaped((NODE, D), f32)]
        + [rim] * 4
        + [shaped((16, 5, 16, D), bf16)] * 2,
        (core, coarse_sender, coarse_receiver),
        (
            same,
            other,
            grad_agg,
            sender,
            receiver,
            edge_latents,
            coarse_edges,
            edge_cotangent,
            coarse_cotangent,
            pre,
            hidden,
            normed,
            scale_r,
            send_rows,
            recv_rows,
            edge_mixer,
            edge_output,
        ),
        [pltpu.VMEM((2, 16, 16, D), f32)],
    )
    got_e = swap(give_e)
    backs = to_neighbours(*backs)
    (total,) = call(chip_sum_kernel, [shaped((16, 8, 16, D), bf16)], (), (keep_e, got_e, keep_n, got_n))
    total = swapped_blocks(total, PLANE)
    (total,) = call(plane_sum_kernel, [shaped((8, 16, D), bf16)], (), (total,))
    total = swapped_blocks(total, ("z",))
    node_grad, mix_part, out_part, node_mix_part, node_out_part = call(
        finish_kernel,
        [
            shaped((NODE, D), bf16),
            shaped((3, 2 * D), f32),
            shaped((1, 2 * D), f32),
            shaped((2, 2 * D), f32),
            shaped((1, 2 * D), f32),
        ],
        (coarse_row, halo_send),
        (total, base, local, *backs),
        [pltpu.VMEM((NODE, D), f32), pltpu.VMEM((RIM, D), f32)],
    )
    return (
        node_update,
        update,
        cupdate,
        node_grad,
        grad,
        cgrad,
        mix_part,
        out_part.reshape(-1),
        node_mix_part,
        node_out_part.reshape(-1),
    )


def solution(mesh):
    fine = Mesh(np.asarray(mesh.devices).reshape(SHAPE), ALL)
    rows = P(ALL, None)
    flat = P(ALL)
    in_specs = (
        rows,
        rows,
        rows,
        flat,
        flat,
        P(ALL, None, None),
        flat,
        flat,
        flat,
        P(),
        P(),
        P(),
        P(),
        rows,
        rows,
        rows,
    )
    out_specs = (rows, rows, rows, rows, rows, rows, P(None, ALL), flat, P(None, ALL), flat)
    return jax.shard_map(shards, mesh=fine, in_specs=in_specs, out_specs=out_specs, check_vma=False)
```

```python
import jax
import jax.numpy as jnp
import numpy as np
from jax import lax
from jax.experimental import pallas as pl
from jax.experimental.pallas import tpu as pltpu
from jax.sharding import Mesh
from jax.sharding import PartitionSpec as P

epsilon = 1e-05
bf16 = jnp.bfloat16
f32 = jnp.float32

ALL = ("xhi", "z", "core", "xlo", "y")
SHAPE = (2, 8, 2, 2, 4)
LON = ("xhi", "z", "core")
LAT = ("xlo", "y")
CHIPS = ("xhi", "z", "xlo", "y")
D = 512
NODE = 32
EDGE = 256
CEDGE = 8
RIM = 8
PAIR = 2 * CEDGE
TABLE = NODE + 4 * RIM


def dot(left, right):
    return lax.dot_general(left, right, (((1,), (0,)), ((), ())), preferred_element_type=f32)


def dot_nt(left, right):
    return lax.dot_general(left, right, (((1,), (1,)), ((), ())), preferred_element_type=f32)


def dot_tn(left, right):
    return lax.dot_general(left, right, (((0,), (0,)), ((), ())), preferred_element_type=f32)


def sigmoid(v):
    return 1.0 / (1.0 + jnp.exp(-v))


def normalize(values):
    center = values - jnp.mean(values, -1, keepdims=True)
    spread = jnp.mean(center * center, -1, keepdims=True)
    scale_r = lax.rsqrt(spread + epsilon)
    return (center * scale_r, scale_r)


def normalize_back(normed, scale_r, incoming):
    mean_g = jnp.mean(incoming, -1, keepdims=True)
    mean_gy = jnp.mean(incoming * normed, -1, keepdims=True)
    return scale_r * (incoming - mean_g - normed * mean_gy)


def swish_slope(values):
    sigma = sigmoid(values)
    return sigma * (1.0 + values * (1.0 - sigma))


def pick_t(count, targets):
    shape = (count, targets.shape[1])
    hit = lax.broadcasted_iota(jnp.int32, shape, 0) == targets
    return jnp.where(hit, 1.0, 0.0).astype(bf16)


def order_matrix(core, first, count):
    wide = (count, 128)
    p = lax.broadcasted_iota(jnp.int32, wide, 0) + first
    side = lax.bitwise_xor(p >> 8, core)
    f = (((p >> 1) & 15) << 5) + (side << 4) + (((p >> 5) & 7) << 1) + (p & 1)
    lane = lax.broadcasted_iota(jnp.int32, wide, 1)
    parts = [jnp.where(f == lane + 128 * j, 1.0, 0.0).astype(bf16) for j in range(D // 128)]
    return jnp.concatenate(parts, axis=1)


def fold(row):
    return jnp.concatenate([row[:, 128 * j : 128 * (j + 1)] for j in range(4)], axis=0)


def unfold(block):
    return jnp.concatenate([block[j : j + 1, :] for j in range(4)], axis=1)


def chip_of(c):
    return (c >> 5) * 8 + ((c >> 1) & 7)


def side_of(c):
    return (c >> 4) & 1


def coarse_pick(same_ref, other_ref, core, c):
    chip = chip_of(c)
    here = (side_of(c) == core).astype(f32)
    block = same_ref[chip].astype(f32) * here + other_ref[chip].astype(f32) * (1.0 - here)
    low = ((c & 1) == 0).astype(f32)
    return unfold(block[0:4] * low + block[4:8] * (1.0 - low))


def partner_lists(core, odd):
    return (1 - core, core, 3 - odd, 2 + odd)


def chosen(flag, one, zero):
    flag = flag.astype(f32)
    return one * flag + zero * (1.0 - flag)


def start_kernel(core_ref, odd_ref, core_row_ref, halo_ref, nodes_ref, h0, h1, h2, h3, spread_ref, table, picked):
    table[...] = nodes_ref[...].astype(f32)
    for k, out in zip(partner_lists(core_ref[0], odd_ref[0]), (h0, h1, h2, h3)):
        for h in range(RIM):
            picked[h : h + 1, :] = table[pl.ds(halo_ref[0, k, h], 1), :]
        out[...] = picked[...].astype(bf16)
    rows = [fold(table[pl.ds(core_row_ref[r], 1), :]) for r in range(2)]
    block = jnp.concatenate(rows, axis=0).astype(bf16)
    spread_ref[...] = jnp.broadcast_to(block[None], spread_ref.shape)


def edge_forward(send, recv, rows, mixer_ref, output_ref, pre_ref, hidden_ref, normed_ref, scale_ref):
    pre = dot(send, mixer_ref[0]) + dot(recv, mixer_ref[1]) + dot(rows, mixer_ref[2])
    pre_ref[...] = pre
    hidden = (pre * sigmoid(pre)).astype(bf16)
    hidden_ref[...] = hidden
    normed, scale_r = normalize(dot(hidden, output_ref[...]))
    normed_ref[...] = normed
    scale_ref[...] = jnp.broadcast_to(scale_r, scale_ref.shape)
    return normed.astype(bf16)


def fine_forward_kernel(
    ready,
    core_ref,
    odd_ref,
    nodes_ref,
    sender_ref,
    receiver_ref,
    edges_ref,
    mixer_ref,
    output_ref,
    h0,
    h1,
    h2,
    h3,
    update_ref,
    agg_ref,
    send_ref,
    recv_ref,
    *kept,
):
    nodes = nodes_ref[...]
    core, odd = core_ref[0], odd_ref[0]
    a, b, c, d = [h[...].astype(f32) for h in (h0, h1, h2, h3)]
    rims = [chosen(core, a, b), chosen(core, b, a), chosen(odd, c, d), chosen(odd, d, c)]
    table = jnp.concatenate([nodes.astype(f32)] + rims, axis=0).astype(bf16)
    into_t = pick_t(NODE, receiver_ref[...])
    send = dot_tn(pick_t(TABLE, sender_ref[...]), table).astype(bf16)
    recv = dot_tn(into_t, nodes).astype(bf16)
    send_ref[...] = send
    recv_ref[...] = recv
    ready()
    edges = edges_ref[...]
    message = edge_forward(send, recv, edges, mixer_ref, output_ref, *kept)
    update_ref[...] = (edges.astype(f32) + message.astype(f32)).astype(bf16)
    agg_ref[...] = dot(into_t, message)


def coarse_forward_kernel(
    ready,
    core_ref,
    csend_ref,
    crecv_ref,
    mine_ref,
    cot_ref,
    mixer_ref,
    output_ref,
    sib_send_ref,
    sib_recv_ref,
    sib_ref,
    sib_cot_ref,
    same_ref,
    other_ref,
    cupdate_ref,
    rows_ref,
    sums_ref,
    lists_ref,
    pair_cot_ref,
    send_ref,
    recv_ref,
    pre_ref,
    hidden_ref,
    normed_ref,
    scale_ref,
    total,
):
    core = core_ref[0]
    for index_refs, out in (((csend_ref, sib_send_ref), send_ref), ((crecv_ref, sib_recv_ref), recv_ref)):
        picked = [coarse_pick(same_ref, other_ref, core, ref[e]) for ref in index_refs for e in range(CEDGE)]
        out[...] = jnp.concatenate(picked, axis=0).astype(bf16)
    for row, ref in enumerate((csend_ref, sib_send_ref, crecv_ref, sib_recv_ref)):
        for e in range(CEDGE):
            lists_ref[row, e] = ref[e]
    pair_cot_ref[...] = jnp.concatenate([cot_ref[...].astype(f32), sib_cot_ref[...].astype(f32)], axis=0)
    wide = jnp.concatenate([mine_ref[...].astype(f32), sib_ref[...].astype(f32)], axis=0)
    rows = wide.astype(bf16)
    rows_ref[...] = rows
    ready()
    kept = (pre_ref, hidden_ref, normed_ref, scale_ref)
    message = edge_forward(send_ref[...], recv_ref[...], rows, mixer_ref, output_ref, *kept).astype(f32)
    cupdate_ref[...] = (wide + message)[0:CEDGE].astype(bf16)
    total[...] = jnp.zeros_like(total)
    for side, index_ref in enumerate((crecv_ref, sib_recv_ref)):
        for e in range(CEDGE):
            c = index_ref[e]
            here = (side_of(c) == core).astype(f32)
            low = ((c & 1) == 0).astype(f32)
            at = side * CEDGE + e
            piece = fold(message[at : at + 1, :])
            chip = chip_of(c)
            block = jnp.concatenate([piece * (here * low), piece * (here * (1.0 - low))], axis=0)
            total[chip] = total[chip] + block
    sums_ref[...] = total[...].astype(bf16)


def put_halves(keep_ref, give_ref, slot, grad):
    keep_ref[:, slot] = grad[0 : D // 2].astype(bf16).reshape(8, 32, D)
    give_ref[:, slot] = grad[D // 2 : D].astype(bf16).reshape(8, 32, D)


def node_kernel(
    coarse_row_ref,
    nodes_ref,
    mixer_ref,
    output_ref,
    cot_ref,
    sums_ref,
    agg_ref,
    update_ref,
    rounded_ref,
    hidden_ref,
    grad_update_ref,
    grad_pre_ref,
    grad_agg_ref,
    spread_ref,
):
    owned = jnp.sum(sums_ref[...].astype(f32), axis=0)
    place = lax.broadcasted_iota(jnp.int32, (NODE, D), 0)
    aggregate = agg_ref[...]
    for r in range(2):
        row = unfold(owned[4 * r : 4 * r + 4])
        aggregate = aggregate + jnp.where(place == coarse_row_ref[r], row, 0.0)
    rounded = aggregate.astype(bf16)
    rounded_ref[...] = rounded
    nodes = nodes_ref[...]
    cot = cot_ref[...].astype(f32)
    pre = dot(nodes, mixer_ref[0]) + dot(rounded, mixer_ref[1])
    hidden = (pre * sigmoid(pre)).astype(bf16)
    hidden_ref[...] = hidden
    normed, scale_r = normalize(dot(hidden, output_ref[...]))
    update_ref[...] = (nodes.astype(f32) + normed).astype(bf16)
    grad_update = normalize_back(normed, scale_r, cot).astype(bf16)
    grad_update_ref[...] = grad_update
    grad_pre = (dot_nt(grad_update, output_ref[...]) * swish_slope(pre)).astype(bf16)
    grad_pre_ref[...] = grad_pre
    grad_agg = dot_nt(grad_pre, mixer_ref[1]).astype(bf16)
    grad_agg_ref[...] = grad_agg
    wide = grad_agg.astype(f32)
    rows = []
    for r in range(2):
        row = jnp.sum(jnp.where(place == coarse_row_ref[r], wide, 0.0), axis=0, keepdims=True)
        rows.append(fold(row))
    block = jnp.concatenate(rows, axis=0).astype(bf16)
    spread_ref[...] = jnp.broadcast_to(block[None], spread_ref.shape)


def node_weights_kernel(
    core_ref, nodes_ref, cot_ref, mixer_ref, rounded_ref, hidden_ref, grad_update_ref, grad_pre_ref, base_ref, keep_ref, give_ref
):
    grad_pre = grad_pre_ref[...]
    base_ref[...] = cot_ref[...].astype(f32) + dot_nt(grad_pre, mixer_ref[0])
    order = order_matrix(core_ref[0], 0, D)
    for slot, (left, right) in enumerate(
        ((nodes_ref, grad_pre), (rounded_ref, grad_pre), (hidden_ref, grad_update_ref[...]))
    ):
        put_halves(keep_ref, give_ref, slot, dot(dot_nt(order, left[...]).astype(bf16), right))


def fine_backward_kernel(
    ready,
    core_ref,
    receiver_ref,
    cot_ref,
    pre_ref,
    normed_ref,
    scale_ref,
    output_ref,
    edges_ref,
    send_ref,
    recv_ref,
    hidden_ref,
    grad_agg_ref,
    grad_act_ref,
    keep_ref,
    give_ref,
):
    into_t = pick_t(NODE, receiver_ref[...])
    incoming = dot_tn(into_t, grad_agg_ref[...]) + cot_ref[...].astype(f32)
    grad_pre = normalize_back(normed_ref[...], scale_ref[:, 0:1], incoming).astype(bf16)
    grad_act = (dot_nt(grad_pre, output_ref[...]) * swish_slope(pre_ref[...])).astype(bf16)
    grad_act_ref[...] = grad_act
    order = order_matrix(core_ref[0], 0, D)
    ready()
    for slot, (left, right) in enumerate(
        ((send_ref, grad_act), (recv_ref, grad_act), (edges_ref, grad_act), (hidden_ref, grad_pre))
    ):
        put_halves(keep_ref, give_ref, slot, dot(dot_nt(order, left[...]).astype(bf16), right))


def fine_inputs_kernel(
    core_ref, odd_ref, sender_ref, receiver_ref, cot_ref, mixer_ref, grad_act_ref, grad_ref, local_ref, g0, g1, g2, g3
):
    into_t = pick_t(NODE, receiver_ref[...])
    from_t = pick_t(TABLE, sender_ref[...])
    grad_act = grad_act_ref[...]
    to_sender = dot_nt(dot(from_t, grad_act).astype(bf16), mixer_ref[0])
    to_receiver = dot_nt(dot(into_t, grad_act).astype(bf16), mixer_ref[1])
    local_ref[...] = to_sender[0:NODE] + to_receiver
    core, odd = core_ref[0], odd_ref[0]
    a, b, c, d = [to_sender[NODE + RIM * k : NODE + RIM * (k + 1)] for k in range(4)]
    rims = [chosen(core, a, b), chosen(core, b, a), chosen(odd, c, d), chosen(odd, d, c)]
    for rim, out in zip(rims, (g0, g1, g2, g3)):
        out[...] = rim.astype(bf16)
    grad_ref[...] = (cot_ref[...].astype(f32) + dot_nt(grad_act, mixer_ref[2])).astype(bf16)


def coarse_backward_kernel(
    ready,
    core_ref,
    lists_ref,
    cot_ref,
    rows_ref,
    send_ref,
    recv_ref,
    pre_ref,
    hidden_ref,
    normed_ref,
    scale_ref,
    mixer_ref,
    output_ref,
    keep_f,
    keep_n,
    got_f,
    got_n,
    same_ref,
    other_ref,
    cgrad_ref,
    out_ref,
    spread,
):
    core = core_ref[0]
    picked = [coarse_pick(same_ref, other_ref, core, lists_ref[2 + e // CEDGE, e % CEDGE]) for e in range(PAIR)]
    cot = cot_ref[...]
    incoming = jnp.concatenate(picked, axis=0) + cot
    grad_pre = normalize_back(normed_ref[...], scale_ref[:, 0:1], incoming).astype(bf16)
    grad_act = (dot_nt(grad_pre, output_ref[...]) * swish_slope(pre_ref[...])).astype(bf16)
    cgrad_ref[...] = (cot + dot_nt(grad_act, mixer_ref[2]))[0:CEDGE].astype(bf16)

    spread[...] = jnp.zeros_like(spread)
    to_sender = dot_nt(grad_act, mixer_ref[0])
    to_receiver = dot_nt(grad_act, mixer_ref[1])
    for first, grads in ((0, to_sender), (2, to_receiver)):
        for e in range(PAIR):
            c = lists_ref[first + e // CEDGE, e % CEDGE]
            here = (side_of(c) == core).astype(f32)
            band = (c >> 1) & 7
            at = pl.ds((c >> 5) * 2 + (c & 1), 1)
            spread[band, at, :] = spread[band, at, :] + grads[e : e + 1, :] * here
    out_ref[:, 4] = spread[...].astype(bf16)

    order = order_matrix(core, 0, D // 2)
    for slot, (left, right) in enumerate(
        ((send_ref, grad_act), (recv_ref, grad_act), (rows_ref, grad_act), (hidden_ref, grad_pre))
    ):
        if slot == 0:
            ready()
        term = dot(dot_nt(order, left[...]).astype(bf16), right).reshape(8, 32, D)
        out_ref[:, slot] = (term + keep_f[:, slot].astype(f32) + got_f[:, slot].astype(f32)).astype(bf16)
    for slot in range(3):
        out_ref[:, 5 + slot] = (keep_n[:, slot].astype(f32) + got_n[:, slot].astype(f32)).astype(bf16)


def band_sum_kernel(in_ref, out_ref):
    total = in_ref[0].astype(f32)
    for d in range(1, 8):
        total = total + in_ref[d].astype(f32)
    total = total.reshape(256, D).astype(bf16)
    place = lax.broadcasted_iota(jnp.int32, (256, 256), 0)
    source = ((place >> 1) & 7) * 32 + (place >> 4) * 2 + (place & 1)
    hit = source == lax.broadcasted_iota(jnp.int32, (256, 256), 1)
    ordered = dot(jnp.where(hit, 1.0, 0.0).astype(bf16), total).astype(bf16)
    out_ref[...] = ordered.reshape(16, 16, D)


def finish_kernel(
    core_ref,
    odd_ref,
    coarse_row_ref,
    halo_ref,
    base_ref,
    local_ref,
    sums_ref,
    r0,
    r1,
    r2,
    r3,
    node_grad_ref,
    mix_ref,
    out_ref,
    node_mix_ref,
    node_out_ref,
    total,
    back,
):
    owned = jnp.sum(sums_ref[...].astype(f32), axis=0)
    total[...] = base_ref[...] + local_ref[...]
    for k, got in zip(partner_lists(core_ref[0], odd_ref[0]), (r0, r1, r2, r3)):
        back[...] = got[...].astype(f32)
        for h in range(RIM):
            at = pl.ds(halo_ref[0, k, h], 1)
            total[at, :] = total[at, :] + back[h : h + 1, :]
    for r in range(2):
        at = pl.ds(coarse_row_ref[r], 1)
        total[at, :] = total[at, :] + owned[8 + r : 9 + r]
        wide = slice(D * r, D * (r + 1))
        for a in range(3):
            mix_ref[a : a + 1, wide] = owned[2 * a + r : 2 * a + r + 1]
        out_ref[:, wide] = owned[6 + r : 7 + r]
        for a in range(2):
            node_mix_ref[a : a + 1, wide] = owned[10 + 2 * a + r : 11 + 2 * a + r]
        node_out_ref[:, wide] = owned[14 + r : 15 + r]
    node_grad_ref[...] = total[...].astype(bf16)


def call(kernel, outs, scalars, far, near, scratch=(), us=1, late=0):
    hbm = pl.BlockSpec(memory_space=pltpu.HBM)

    def space(x):
        return pl.BlockSpec(memory_space=pltpu.SMEM if x.dtype == jnp.int32 else pltpu.VMEM)

    fetched = [pltpu.with_memory_space_constraint(x, pltpu.HBM) for x in (*scalars, *far)]
    held = [pltpu.SMEM(x.shape, x.dtype) for x in scalars] + [pltpu.VMEM(x.shape, x.dtype) for x in far]
    count = len(fetched)

    def body(*refs):
        sources, refs = refs[:count], refs[count:]
        passed, refs = refs[: len(near) + len(outs)], refs[len(near) + len(outs) :]
        slots, sems, rest = refs[:count], refs[count], refs[count + 1 :]
        copies = [pltpu.make_async_copy(x, y, sems.at[i]) for i, (x, y) in enumerate(zip(sources, slots))]
        for copy in copies:
            copy.start()
        for copy in copies[: count - late]:
            copy.wait()

        def ready():
            for copy in copies[count - late :]:
                copy.wait()

        kernel(*([ready] if late else []), *slots, *passed, *rest)

    moved = sum(int(np.prod(x.shape)) * x.dtype.itemsize for x in (*fetched, *near, *outs))
    return pl.pallas_call(
        body,
        out_shape=outs,
        in_specs=[hbm] * count + [space(x) for x in near],
        out_specs=[space(x) for x in outs],
        scratch_shapes=[*held, pltpu.SemaphoreType.DMA((max(count, 1),)), *scratch],
        compiler_params=pltpu.CompilerParams(vmem_limit_bytes=24 * 2**20),
        cost_estimate=pl.CostEstimate(flops=us * 1_150_000_000, bytes_accessed=moved, transcendentals=0),
    )(*fetched, *near)


def shaped(shape, dtype):
    return jax.ShapeDtypeStruct(shape, dtype)


def stored(shape, dtype):
    return pltpu.HBM(shape, dtype)


def swap(x):
    return lax.ppermute(x, "core", [(0, 1), (1, 0)])


def to_partners(a, b, c, d):
    def exchange(x, axes, pairs):
        return lax.ppermute(x, axes, pairs + [(j, i) for i, j in pairs])

    b = exchange(b, LON, [(i, (i + 1) % 32) for i in range(1, 32, 2)])
    d = exchange(d, LAT, [(i, i + 1) for i in range(1, 7, 2)])
    c = exchange(c, LAT, [(i, i + 1) for i in range(0, 8, 2)])
    return (swap(a), b, c, d)


def swapped_blocks(x, axes):
    return lax.all_to_all(x, axes, 0, 0, tiled=True)


def shards(
    node_latents,
    edge_latents,
    coarse_edges,
    sender,
    receiver,
    halo_send,
    coarse_row,
    coarse_sender,
    coarse_receiver,
    edge_mixer,
    edge_output,
    node_mixer,
    node_output,
    node_cotangent,
    edge_cotangent,
    coarse_cotangent,
):
    core = lax.axis_index("core").astype(jnp.int32).reshape(1)
    odd = (lax.axis_index("y") & 1).astype(jnp.int32).reshape(1)
    sender = sender.reshape(1, EDGE)
    receiver = receiver.reshape(1, EDGE)
    rim = shaped((RIM, D), bf16)
    blocks = shaped((128, 8, 128), bf16)

    def kept(count):
        return [
            stored((count, D), bf16),
            stored((count, D), bf16),
            stored((count, D), f32),
            stored((count, D), bf16),
            stored((count, D), f32),
            stored((count, 128), f32),
        ]

    *rims, spread = call(
        start_kernel,
        [rim] * 4 + [blocks],
        (core, odd, coarse_row, halo_send),
        (node_latents,),
        (),
        [pltpu.VMEM((NODE, D), f32), pltpu.VMEM((RIM, D), f32)],
    )
    same = swapped_blocks(spread, CHIPS)
    rims = to_partners(*rims)
    sib_edges, sib_cot = swap(coarse_edges), swap(coarse_cotangent)
    sib_send, sib_recv = swap(coarse_sender), swap(coarse_receiver)
    same, sib_edges, sib_cot, sib_send, sib_recv, *rims = lax.optimization_barrier(
        (same, sib_edges, sib_cot, sib_send, sib_recv, *rims)
    )
    other = swap(same)
    cupdate, crows, sums, lists, pair_cot, *coarse = call(
        coarse_forward_kernel,
        [
            shaped((CEDGE, D), bf16),
            stored((PAIR, D), bf16),
            blocks,
            stored((4, CEDGE), jnp.int32),
            stored((PAIR, D), f32),
        ]
        + kept(PAIR),
        (core, coarse_sender, coarse_receiver),
        (coarse_edges, coarse_cotangent, edge_mixer, edge_output),
        (sib_send, sib_recv, sib_edges, sib_cot, same, other),
        [pltpu.VMEM((128, 8, 128), f32)],
        us=3,
        late=2,
    )
    sums, *rims = lax.optimization_barrier((sums, *rims))
    sums = swapped_blocks(sums, CHIPS)
    update, agg, *fine = call(
        fine_forward_kernel,
        [shaped((EDGE, D), bf16), shaped((NODE, D), f32)] + kept(EDGE),
        (core, odd),
        (node_latents, sender, receiver, edge_latents, edge_mixer, edge_output),
        rims,
        us=4,
        late=3,
    )

    small = shaped((NODE, D), bf16)
    node_update, *node_kept, grad_agg, spread = call(
        node_kernel,
        [small] * 6 + [blocks],
        (coarse_row,),
        (),
        (node_latents, node_mixer, node_output, node_cotangent, sums, agg),
        us=3,
    )
    same = swapped_blocks(spread, CHIPS)
    base, keep_n, give_n = call(
        node_weights_kernel,
        [stored((NODE, D), f32)] + [stored((8, 3, 32, D), bf16)] * 2,
        (core,),
        (node_latents, node_cotangent, node_mixer),
        node_kept,
        us=3,
    )
    send_rows, recv_rows, pre, hidden, normed, scale_r = fine
    grad_act, keep_f, give_f = call(
        fine_backward_kernel,
        [stored((EDGE, D), bf16)] + [stored((8, 4, 32, D), bf16)] * 2,
        (core,),
        (receiver, edge_cotangent, pre, normed, scale_r, edge_output, edge_latents, send_rows, recv_rows, hidden),
        (grad_agg,),
        us=5,
        late=4,
    )
    same, keep_f, give_f, keep_n, give_n = lax.optimization_barrier((same, keep_f, give_f, keep_n, give_n))
    other = swap(same)
    got_f = swap(give_f)
    got_n = swap(give_n)
    cgrad, total = call(
        coarse_backward_kernel,
        [shaped((CEDGE, D), bf16), shaped((8, 8, 32, D), bf16)],
        (core, lists),
        (pair_cot, crows, *coarse, edge_mixer, edge_output, keep_f, keep_n),
        (got_f, got_n, same, other),
        [pltpu.VMEM((8, 32, D), f32)],
        us=4,
        late=2,
    )
    total, grad_act = lax.optimization_barrier((total, grad_act))
    total = swapped_blocks(total, LAT)
    grad, local, *backs = call(
        fine_inputs_kernel,
        [shaped((EDGE, D), bf16), stored((NODE, D), f32)] + [rim] * 4,
        (core, odd),
        (sender, receiver, edge_cotangent, edge_mixer, grad_act),
        (),
        us=4,
    )
    total, *backs = lax.optimization_barrier((total, *backs))
    (total,) = call(band_sum_kernel, [shaped((16, 16, D), bf16)], (), (), (total,), us=1)
    total, *backs = lax.optimization_barrier((total, *backs))
    total = swapped_blocks(total, ("xhi", "z"))
    backs = to_partners(*backs)
    node_grad, mix_part, out_part, node_mix_part, node_out_part = call(
        finish_kernel,
        [
            shaped((NODE, D), bf16),
            shaped((3, 2 * D), f32),
            shaped((1, 2 * D), f32),
            shaped((2, 2 * D), f32),
            shaped((1, 2 * D), f32),
        ],
        (core, odd, coarse_row, halo_send),
        (base, local),
        (total, *backs),
        [pltpu.VMEM((NODE, D), f32), pltpu.VMEM((RIM, D), f32)],
    )
    return (
        node_update,
        update,
        cupdate,
        node_grad,
        grad,
        cgrad,
        mix_part,
        out_part.reshape(-1),
        node_mix_part,
        node_out_part.reshape(-1),
    )


def solution(mesh):
    fine = Mesh(np.asarray(mesh.devices).reshape(SHAPE), ALL)
    rows = P(ALL, None)
    flat = P(ALL)
    in_specs = (
        rows,
        rows,
        rows,
        flat,
        flat,
        P(ALL, None, None),
        flat,
        flat,
        flat,
        P(),
        P(),
        P(),
        P(),
        rows,
        rows,
        rows,
    )
    out_specs = (rows, rows, rows, rows, rows, rows, P(None, ALL), flat, P(None, ALL), flat)
    return jax.shard_map(shards, mesh=fine, in_specs=in_specs, out_specs=out_specs, check_vma=False)
```

```python
import jax
import jax.numpy as jnp
import numpy as np
from jax import lax
from jax.experimental import pallas as pl
from jax.experimental.pallas import tpu as pltpu
from jax.sharding import Mesh
from jax.sharding import PartitionSpec as P

epsilon = 1e-05
bf16 = jnp.bfloat16
f32 = jnp.float32

ALL = ("xhi", "z", "core", "xlo", "y")
SHAPE = (2, 8, 2, 2, 4)
LON = ("xhi", "z", "core")
LAT = ("xlo", "y")
CHIPS = ("xhi", "z", "xlo", "y")
D = 512
NODE = 32
EDGE = 256
CEDGE = 8
RIM = 8
PAIR = 2 * CEDGE
TABLE = NODE + 4 * RIM


def dot(left, right):
    return lax.dot_general(left, right, (((1,), (0,)), ((), ())), preferred_element_type=f32)


def dot_nt(left, right):
    return lax.dot_general(left, right, (((1,), (1,)), ((), ())), preferred_element_type=f32)


def dot_tn(left, right):
    return lax.dot_general(left, right, (((0,), (0,)), ((), ())), preferred_element_type=f32)


def sigmoid(v):
    return 1.0 / (1.0 + jnp.exp(-v))


def normalize(values):
    center = values - jnp.mean(values, -1, keepdims=True)
    spread = jnp.mean(center * center, -1, keepdims=True)
    scale_r = lax.rsqrt(spread + epsilon)
    return (center * scale_r, scale_r)


def normalize_back(normed, scale_r, incoming):
    mean_g = jnp.mean(incoming, -1, keepdims=True)
    mean_gy = jnp.mean(incoming * normed, -1, keepdims=True)
    return scale_r * (incoming - mean_g - normed * mean_gy)


def swish_slope(values):
    sigma = sigmoid(values)
    return sigma * (1.0 + values * (1.0 - sigma))


def pick_t(count, targets):
    shape = (count, targets.shape[1])
    hit = lax.broadcasted_iota(jnp.int32, shape, 0) == targets
    return jnp.where(hit, 1.0, 0.0).astype(bf16)


def order_matrix(core, first, count):
    wide = (count, 128)
    p = lax.broadcasted_iota(jnp.int32, wide, 0) + first
    side = lax.bitwise_xor(p >> 8, core)
    f = (((p >> 1) & 15) << 5) + (side << 4) + (((p >> 5) & 7) << 1) + (p & 1)
    lane = lax.broadcasted_iota(jnp.int32, wide, 1)
    parts = [jnp.where(f == lane + 128 * j, 1.0, 0.0).astype(bf16) for j in range(D // 128)]
    return jnp.concatenate(parts, axis=1)


def fold(row):
    return jnp.concatenate([row[:, 128 * j : 128 * (j + 1)] for j in range(4)], axis=0)


def unfold(block):
    return jnp.concatenate([block[j : j + 1, :] for j in range(4)], axis=1)


def chip_of(c):
    return (c >> 5) * 8 + ((c >> 1) & 7)


def side_of(c):
    return (c >> 4) & 1


def coarse_ends(lists):
    return [(lists[:, 2 * k : 2 * k + 1] * 32.0 + lists[:, 2 * k + 1 : 2 * k + 2]).astype(jnp.int32) for k in range(2)]


def coarse_pick(c, core):
    shape = (c.shape[0], D)
    place = lax.bitwise_xor(side_of(c), core) * 256 + chip_of(c) * 2 + (c & 1)
    return jnp.where(lax.broadcasted_iota(jnp.int32, shape, 1) == place, 1.0, 0.0).astype(bf16)


def coarse_rows(same, other, table):
    table[0:1024, :] = same.astype(f32).reshape(1024, 128)
    table[1024:2048, :] = other.astype(f32).reshape(1024, 128)
    return jnp.concatenate([table[pl.ds(j, 512, stride=4), :] for j in range(4)], axis=1).astype(bf16)


def partner_lists(core, odd):
    return (1 - core, core, 3 - odd, 2 + odd)


def chosen(flag, one, zero):
    flag = flag.astype(f32)
    return one * flag + zero * (1.0 - flag)


def start_kernel(
    core_ref,
    odd_ref,
    core_row_ref,
    halo_ref,
    csend_ref,
    crecv_ref,
    nodes_ref,
    cedges_ref,
    ccot_ref,
    h0,
    h1,
    h2,
    h3,
    spread_ref,
    own_ref,
    table,
    picked,
    own,
):
    table[...] = nodes_ref[...].astype(f32)
    rows = [fold(table[pl.ds(core_row_ref[r], 1), :]) for r in range(2)]
    block = jnp.concatenate(rows, axis=0).astype(bf16)
    spread_ref[...] = jnp.broadcast_to(block[None], spread_ref.shape)
    own[0:CEDGE, :] = cedges_ref[...].astype(f32)
    own[CEDGE : 2 * CEDGE, :] = ccot_ref[...].astype(f32)
    own[2 * CEDGE :, :] = jnp.zeros((2 * CEDGE, D), f32)
    lane = lax.broadcasted_iota(jnp.int32, (1, 128), 1)
    for e in range(CEDGE):
        row = jnp.zeros((1, 128), f32)
        for at, c in enumerate((csend_ref[e], crecv_ref[e])):
            row = jnp.where(lane == 2 * at, (c >> 5).astype(f32), row)
            row = jnp.where(lane == 2 * at + 1, (c & 31).astype(f32), row)
        own[2 * CEDGE + e : 2 * CEDGE + e + 1, 0:128] = row
    own_ref[...] = own[...].astype(bf16)
    for k, out in zip(partner_lists(core_ref[0], odd_ref[0]), (h0, h1, h2, h3)):
        for h in range(RIM):
            picked[h : h + 1, :] = table[pl.ds(halo_ref[0, k, h], 1), :]
        out[...] = picked[...].astype(bf16)


def edge_forward(send, recv, rows, mixer_ref, output_ref):
    pre = dot(send, mixer_ref[0]) + dot(recv, mixer_ref[1]) + dot(rows, mixer_ref[2])
    hidden = (pre * sigmoid(pre)).astype(bf16)
    normed, scale_r = normalize(dot(hidden, output_ref[...]))
    return pre, hidden, normed, scale_r


def fine_forward_kernel(
    ready,
    core_ref,
    odd_ref,
    nodes_ref,
    sender_ref,
    receiver_ref,
    edges_ref,
    mixer_ref,
    output_ref,
    h0,
    h1,
    h2,
    h3,
    same_ref,
    other_ref,
    update_ref,
    agg_ref,
    gathered_ref,
    send_ref,
    recv_ref,
    pre_ref,
    hidden_ref,
    normed_ref,
    scale_ref,
):
    nodes = nodes_ref[...]
    gathered_ref[0] = same_ref[...]
    gathered_ref[1] = other_ref[...]
    core, odd = core_ref[0], odd_ref[0]
    a, b, c, d = [h[...].astype(f32) for h in (h0, h1, h2, h3)]
    rims = [chosen(core, a, b), chosen(core, b, a), chosen(odd, c, d), chosen(odd, d, c)]
    table = jnp.concatenate([nodes.astype(f32)] + rims, axis=0).astype(bf16)
    into_t = pick_t(NODE, receiver_ref[...])
    send = dot_tn(pick_t(TABLE, sender_ref[...]), table).astype(bf16)
    recv = dot_tn(into_t, nodes).astype(bf16)
    send_ref[...] = send
    recv_ref[...] = recv
    ready()
    edges = edges_ref[...]
    pre, hidden, normed, scale_r = edge_forward(send, recv, edges, mixer_ref, output_ref)
    pre_ref[...] = pre
    hidden_ref[...] = hidden
    normed_ref[...] = normed
    scale_ref[...] = jnp.broadcast_to(scale_r, scale_ref.shape)
    message = normed.astype(bf16)
    update_ref[...] = (edges.astype(f32) + message.astype(f32)).astype(bf16)
    agg_ref[...] = dot(into_t, message)


def coarse_forward_kernel(
    ready,
    core_ref,
    mixer_ref,
    output_ref,
    pair_ref,
    same_ref,
    other_ref,
    cupdate_ref,
    sums_ref,
    table,
    total,
):
    core = core_ref[0]
    pair = pair_ref[...].astype(f32)
    rows, _, lists = (
        jnp.concatenate([pair[CEDGE * k : CEDGE * (k + 1)], pair[CEDGE * (k + 4) : CEDGE * (k + 5)]], axis=0) for k in range(3)
    )
    latents = coarse_rows(same_ref[...], other_ref[...], table)
    ends = coarse_ends(lists)
    send, recv = (dot(coarse_pick(c, core), latents).astype(bf16) for c in ends)
    ready()
    _, _, normed, _ = edge_forward(send, recv, rows.astype(bf16), mixer_ref, output_ref)
    message = normed.astype(bf16)
    cupdate_ref[...] = (rows + message.astype(f32))[0:CEDGE].astype(bf16)
    into = dot_tn(coarse_pick(ends[1], core), message)[0 : D // 2]
    for j in range(4):
        total[pl.ds(j, D // 2, stride=4), :] = into[:, 128 * j : 128 * (j + 1)]
    sums_ref[...] = total[...].reshape(128, 8, 128).astype(bf16)


def put_halves(keep_ref, give_ref, slot, grad):
    keep_ref[:, slot] = grad[0 : D // 2].astype(bf16).reshape(8, 32, D)
    give_ref[:, slot] = grad[D // 2 : D].astype(bf16).reshape(8, 32, D)


def node_kernel(
    coarse_row_ref,
    nodes_ref,
    mixer_ref,
    output_ref,
    cot_ref,
    sums_ref,
    agg_ref,
    update_ref,
    rounded_ref,
    hidden_ref,
    grad_update_ref,
    grad_pre_ref,
    grad_agg_ref,
    spread_ref,
):
    owned = jnp.sum(sums_ref[...].astype(f32), axis=0)
    place = lax.broadcasted_iota(jnp.int32, (NODE, D), 0)
    aggregate = agg_ref[...]
    for r in range(2):
        row = unfold(owned[4 * r : 4 * r + 4])
        aggregate = aggregate + jnp.where(place == coarse_row_ref[r], row, 0.0)
    rounded = aggregate.astype(bf16)
    rounded_ref[...] = rounded
    nodes = nodes_ref[...]
    cot = cot_ref[...].astype(f32)
    pre = dot(nodes, mixer_ref[0]) + dot(rounded, mixer_ref[1])
    hidden = (pre * sigmoid(pre)).astype(bf16)
    hidden_ref[...] = hidden
    normed, scale_r = normalize(dot(hidden, output_ref[...]))
    update_ref[...] = (nodes.astype(f32) + normed).astype(bf16)
    grad_update = normalize_back(normed, scale_r, cot).astype(bf16)
    grad_update_ref[...] = grad_update
    grad_pre = (dot_nt(grad_update, output_ref[...]) * swish_slope(pre)).astype(bf16)
    grad_pre_ref[...] = grad_pre
    grad_agg = dot_nt(grad_pre, mixer_ref[1]).astype(bf16)
    grad_agg_ref[...] = grad_agg
    wide = grad_agg.astype(f32)
    rows = []
    for r in range(2):
        row = jnp.sum(jnp.where(place == coarse_row_ref[r], wide, 0.0), axis=0, keepdims=True)
        rows.append(fold(row))
    block = jnp.concatenate(rows, axis=0).astype(bf16)
    spread_ref[...] = jnp.broadcast_to(block[None], spread_ref.shape)


def node_weights_kernel(
    core_ref, nodes_ref, cot_ref, mixer_ref, rounded_ref, hidden_ref, grad_update_ref, grad_pre_ref, base_ref, keep_ref, give_ref
):
    grad_pre = grad_pre_ref[...]
    base_ref[...] = cot_ref[...].astype(f32) + dot_nt(grad_pre, mixer_ref[0])
    order = order_matrix(core_ref[0], 0, D)
    for slot, (left, right) in enumerate(
        ((nodes_ref, grad_pre), (rounded_ref, grad_pre), (hidden_ref, grad_update_ref[...]))
    ):
        put_halves(keep_ref, give_ref, slot, dot(dot_nt(order, left[...]).astype(bf16), right))


def fine_backward_kernel(
    ready,
    core_ref,
    receiver_ref,
    cot_ref,
    pre_ref,
    normed_ref,
    scale_ref,
    output_ref,
    edges_ref,
    send_ref,
    recv_ref,
    hidden_ref,
    grad_agg_ref,
    grad_act_ref,
    keep_ref,
    give_ref,
):
    into_t = pick_t(NODE, receiver_ref[...])
    incoming = dot_tn(into_t, grad_agg_ref[...]) + cot_ref[...].astype(f32)
    grad_pre = normalize_back(normed_ref[...], scale_ref[:, 0:1], incoming).astype(bf16)
    grad_act = (dot_nt(grad_pre, output_ref[...]) * swish_slope(pre_ref[...])).astype(bf16)
    grad_act_ref[...] = grad_act
    order = order_matrix(core_ref[0], 0, D)
    ready()
    for slot, (left, right) in enumerate(
        ((send_ref, grad_act), (recv_ref, grad_act), (edges_ref, grad_act), (hidden_ref, grad_pre))
    ):
        put_halves(keep_ref, give_ref, slot, dot(dot_nt(order, left[...]).astype(bf16), right))


def fine_inputs_kernel(
    core_ref, odd_ref, sender_ref, receiver_ref, cot_ref, mixer_ref, grad_act_ref, grad_ref, local_ref, g0, g1, g2, g3
):
    into_t = pick_t(NODE, receiver_ref[...])
    from_t = pick_t(TABLE, sender_ref[...])
    grad_act = grad_act_ref[...]
    to_sender = dot_nt(dot(from_t, grad_act).astype(bf16), mixer_ref[0])
    to_receiver = dot_nt(dot(into_t, grad_act).astype(bf16), mixer_ref[1])
    local_ref[...] = to_sender[0:NODE] + to_receiver
    core, odd = core_ref[0], odd_ref[0]
    a, b, c, d = [to_sender[NODE + RIM * k : NODE + RIM * (k + 1)] for k in range(4)]
    rims = [chosen(core, a, b), chosen(core, b, a), chosen(odd, c, d), chosen(odd, d, c)]
    for rim, out in zip(rims, (g0, g1, g2, g3)):
        out[...] = rim.astype(bf16)
    grad_ref[...] = (cot_ref[...].astype(f32) + dot_nt(grad_act, mixer_ref[2])).astype(bf16)


def chip_sum_kernel(keep_n, keep_f, got_f, got_n, out_ref):
    for d in range(8):
        out_ref[d, 0:4] = (keep_f[d].astype(f32) + got_f[d].astype(f32)).astype(bf16)
        out_ref[d, 4:7] = (keep_n[d].astype(f32) + got_n[d].astype(f32)).astype(bf16)


def coarse_backward_kernel(
    core_ref,
    band_ref,
    gathered_ref,
    mixer_ref,
    output_ref,
    near_edges_ref,
    far_edges_ref,
    same_ref,
    other_ref,
    cgrad_ref,
    terms_ref,
    table,
):
    core, band = core_ref[0], band_ref[0]

    count = 8 * PAIR
    wide = jnp.concatenate([near_edges_ref[...].astype(f32), far_edges_ref[...].astype(f32)], axis=0)
    wide = wide.reshape(8, 2, 4 * CEDGE, D)
    rows, cot, lists = (
        wide[:, :, CEDGE * k : CEDGE * (k + 1)].reshape(count, D) for k in range(3)
    )
    ends = coarse_ends(lists)

    def pick_owned(c):
        mine = (side_of(c) == core) & (((c >> 1) & 7) == band)
        place = jnp.where(mine, (c >> 5) * 2 + (c & 1), -1)
        hit = lax.broadcasted_iota(jnp.int32, (count, 128), 1) == place
        return jnp.where(hit, 1.0, 0.0).astype(bf16)

    rows = rows.astype(bf16)
    latents = coarse_rows(gathered_ref[0], gathered_ref[1], table)
    send = dot(coarse_pick(ends[0], core), latents).astype(bf16)
    into = coarse_pick(ends[1], core)
    recv = dot(into, latents).astype(bf16)
    pre, hidden, normed, scale_r = edge_forward(send, recv, rows, mixer_ref, output_ref)
    incoming = dot(into, coarse_rows(same_ref[...], other_ref[...], table)) + cot
    grad_pre = normalize_back(normed, scale_r, incoming).astype(bf16)
    grad_act = (dot_nt(grad_pre, output_ref[...]) * swish_slope(pre)).astype(bf16)
    cgrad_ref[...] = (cot[0:PAIR] + dot_nt(grad_act[0:PAIR], mixer_ref[2]))[0:CEDGE].astype(bf16)

    owned = 2 * 16
    by_sender = dot_tn(pick_owned(ends[0]), grad_act)[0:owned].astype(bf16)
    by_receiver = dot_tn(pick_owned(ends[1]), grad_act)[0:owned].astype(bf16)
    terms_ref[4] = dot_nt(by_sender, mixer_ref[0]) + dot_nt(by_receiver, mixer_ref[1])
    p = lax.broadcasted_iota(jnp.int32, (owned, D), 0)
    f = ((p >> 1) << 5) + (core << 4) + (band << 1) + (p & 1)
    order = jnp.where(f == lax.broadcasted_iota(jnp.int32, (owned, D), 1), 1.0, 0.0).astype(bf16)
    for slot, (left, right) in enumerate(((send, grad_act), (recv, grad_act), (rows, grad_act), (hidden, grad_pre))):
        terms_ref[slot] = dot(dot_nt(order, left).astype(bf16), right)


def band_sum_kernel(terms_ref, in_ref, out_ref):
    total = in_ref[0].astype(f32)
    for d in range(1, 8):
        total = total + in_ref[d].astype(f32)
    terms = terms_ref[...]
    total = jnp.concatenate([total[0:4] + terms[0:4], terms[4:5], total[4:7]], axis=0)
    total = total.reshape(256, D).astype(bf16)
    place = lax.broadcasted_iota(jnp.int32, (256, 256), 0)
    source = ((place >> 1) & 7) * 32 + (place >> 4) * 2 + (place & 1)
    hit = source == lax.broadcasted_iota(jnp.int32, (256, 256), 1)
    ordered = dot(jnp.where(hit, 1.0, 0.0).astype(bf16), total).astype(bf16)
    out_ref[...] = ordered.reshape(16, 16, D)


def rim_sum_kernel(core_ref, odd_ref, halo_ref, base_ref, local_ref, r0, r1, r2, r3, near_ref, back):
    near_ref[...] = base_ref[...] + local_ref[...]
    for k, got in zip(partner_lists(core_ref[0], odd_ref[0]), (r0, r1, r2, r3)):
        back[...] = got[...].astype(f32)
        for h in range(RIM):
            at = pl.ds(halo_ref[0, k, h], 1)
            near_ref[at, :] = near_ref[at, :] + back[h : h + 1, :]


def finish_kernel(
    coarse_row_ref,
    sums_ref,
    near_ref,
    node_grad_ref,
    mix_ref,
    out_ref,
    node_mix_ref,
    node_out_ref,
    total,
):
    owned = jnp.sum(sums_ref[...].astype(f32), axis=0)
    total[...] = near_ref[...]
    for r in range(2):
        at = pl.ds(coarse_row_ref[r], 1)
        total[at, :] = total[at, :] + owned[8 + r : 9 + r]
        wide = slice(D * r, D * (r + 1))
        for a in range(3):
            mix_ref[a : a + 1, wide] = owned[2 * a + r : 2 * a + r + 1]
        out_ref[:, wide] = owned[6 + r : 7 + r]
        for a in range(2):
            node_mix_ref[a : a + 1, wide] = owned[10 + 2 * a + r : 11 + 2 * a + r]
        node_out_ref[:, wide] = owned[14 + r : 15 + r]
    node_grad_ref[...] = total[...].astype(bf16)


def call(kernel, outs, scalars, far, near, scratch=(), us=1, late=0):
    hbm = pl.BlockSpec(memory_space=pltpu.HBM)

    def space(x):
        return pl.BlockSpec(memory_space=pltpu.SMEM if x.dtype == jnp.int32 else pltpu.VMEM)

    fetched = [pltpu.with_memory_space_constraint(x, pltpu.HBM) for x in (*scalars, *far)]
    held = [pltpu.SMEM(x.shape, x.dtype) for x in scalars] + [pltpu.VMEM(x.shape, x.dtype) for x in far]
    count = len(fetched)

    def body(*refs):
        sources, refs = refs[:count], refs[count:]
        passed, refs = refs[: len(near) + len(outs)], refs[len(near) + len(outs) :]
        slots, sems, rest = refs[:count], refs[count], refs[count + 1 :]
        copies = [pltpu.make_async_copy(x, y, sems.at[i]) for i, (x, y) in enumerate(zip(sources, slots))]
        for copy in copies:
            copy.start()
        for copy in copies[: count - late]:
            copy.wait()

        def ready():
            for copy in copies[count - late :]:
                copy.wait()

        kernel(*([ready] if late else []), *slots, *passed, *rest)

    moved = sum(int(np.prod(x.shape)) * x.dtype.itemsize for x in (*fetched, *near, *outs))
    return pl.pallas_call(
        body,
        out_shape=outs,
        in_specs=[hbm] * count + [space(x) for x in near],
        out_specs=[space(x) for x in outs],
        scratch_shapes=[*held, pltpu.SemaphoreType.DMA((max(count, 1),)), *scratch],
        compiler_params=pltpu.CompilerParams(vmem_limit_bytes=24 * 2**20),
        cost_estimate=pl.CostEstimate(flops=us * 1_150_000_000, bytes_accessed=moved, transcendentals=0),
    )(*fetched, *near)


def shaped(shape, dtype):
    return jax.ShapeDtypeStruct(shape, dtype)


def stored(shape, dtype):
    return pltpu.HBM(shape, dtype)


def swap(x):
    return lax.ppermute(x, "core", [(0, 1), (1, 0)])


def to_partners(a, b, c, d):
    def exchange(x, axes, pairs):
        return lax.ppermute(x, axes, pairs + [(j, i) for i, j in pairs])

    b = exchange(b, LON, [(i, (i + 1) % 32) for i in range(1, 32, 2)])
    d = exchange(d, LAT, [(i, i + 1) for i in range(1, 7, 2)])
    c = exchange(c, LAT, [(i, i + 1) for i in range(0, 8, 2)])
    return (swap(a), b, c, d)


def across(x, mask):
    return lax.ppermute(x, LAT, [(i, i ^ mask) for i in range(8)])


def doubled(x, mask):
    return jnp.concatenate([x, across(x, mask)], axis=0)


def swapped_blocks(x, axes):
    return lax.all_to_all(x, axes, 0, 0, tiled=True)


def shards(
    node_latents,
    edge_latents,
    coarse_edges,
    sender,
    receiver,
    halo_send,
    coarse_row,
    coarse_sender,
    coarse_receiver,
    edge_mixer,
    edge_output,
    node_mixer,
    node_output,
    node_cotangent,
    edge_cotangent,
    coarse_cotangent,
):
    core = lax.axis_index("core").astype(jnp.int32).reshape(1)
    odd = (lax.axis_index("y") & 1).astype(jnp.int32).reshape(1)
    band = lax.axis_index(LAT).astype(jnp.int32).reshape(1)
    sender = sender.reshape(1, EDGE)
    receiver = receiver.reshape(1, EDGE)
    rim = shaped((RIM, D), bf16)
    blocks = shaped((128, 8, 128), bf16)

    def kept(count):
        return [
            stored((count, D), bf16),
            stored((count, D), bf16),
            stored((count, D), f32),
            stored((count, D), bf16),
            stored((count, D), f32),
            stored((count, 128), f32),
        ]

    *rims, spread, own = call(
        start_kernel,
        [rim] * 4 + [blocks, shaped((4 * CEDGE, D), bf16)],
        (core, odd, coarse_row, halo_send, coarse_sender, coarse_receiver),
        (node_latents, coarse_edges, coarse_cotangent),
        (),
        [pltpu.VMEM((NODE, D), f32), pltpu.VMEM((RIM, D), f32), pltpu.VMEM((4 * CEDGE, D), f32)],
    )
    same = swapped_blocks(spread, CHIPS)
    pair = jnp.concatenate([own, swap(own)], axis=0)
    rims = to_partners(*rims)
    known = doubled(pair, 1)
    same, pair, known, *rims = lax.optimization_barrier((same, pair, known, *rims))
    other = swap(same)
    cupdate, sums = call(
        coarse_forward_kernel,
        [shaped((CEDGE, D), bf16), blocks],
        (core,),
        (edge_mixer, edge_output),
        (pair, same, other),
        [pltpu.VMEM((2048, 128), f32), pltpu.VMEM((1024, 128), f32)],
        us=3,
        late=2,
    )
    sums, known, *rims = lax.optimization_barrier((sums, known, *rims))
    sums = swapped_blocks(sums, CHIPS)
    known = doubled(known, 2)
    update, agg, gathered, *fine = call(
        fine_forward_kernel,
        [shaped((EDGE, D), bf16), shaped((NODE, D), f32), stored((2, 128, 8, 128), bf16)] + kept(EDGE),
        (core, odd),
        (node_latents, sender, receiver, edge_latents, edge_mixer, edge_output),
        (*rims, same, other),
        us=4,
        late=3,
    )
    sums, known, agg = lax.optimization_barrier((sums, known, agg))
    small = shaped((NODE, D), bf16)
    node_update, *node_kept, grad_agg, spread = call(
        node_kernel,
        [small] + [stored((NODE, D), bf16)] * 4 + [small, blocks],
        (coarse_row,),
        (),
        (node_latents, node_mixer, node_output, node_cotangent, sums, agg),
        us=3,
    )
    spread, known, grad_agg = lax.optimization_barrier((spread, known, grad_agg))
    same = swapped_blocks(spread, CHIPS)
    far_half = across(known, 4)
    base, keep_n, give_n = call(
        node_weights_kernel,
        [stored((NODE, D), f32)] + [shaped((8, 3, 32, D), bf16)] * 2,
        (core,),
        (node_latents, node_cotangent, node_mixer, *node_kept),
        (),
        us=3,
    )
    send_rows, recv_rows, pre, hidden, normed, scale_r = fine
    grad_act, keep_f, give_f = call(
        fine_backward_kernel,
        [stored((EDGE, D), bf16)] + [shaped((8, 4, 32, D), bf16)] * 2,
        (core,),
        (receiver, edge_cotangent, pre, normed, scale_r, edge_output, edge_latents, send_rows, recv_rows, hidden),
        (grad_agg,),
        us=5,
        late=4,
    )
    same, keep_f, give_f, keep_n, give_n, far_half = lax.optimization_barrier(
        (same, keep_f, give_f, keep_n, give_n, far_half)
    )
    (total,) = call(
        chip_sum_kernel,
        [shaped((8, 7, 32, D), bf16)],
        (),
        (),
        (keep_n, keep_f, swap(give_f), swap(give_n)),
    )
    total, same, grad_act = lax.optimization_barrier((total, same, grad_act))
    total = swapped_blocks(total, LAT)
    other = swap(same)
    cgrad, terms = call(
        coarse_backward_kernel,
        [shaped((CEDGE, D), bf16), shaped((5, 32, D), f32)],
        (core, band),
        (gathered, edge_mixer, edge_output),
        (known, far_half, same, other),
        [pltpu.VMEM((2048, 128), f32)],
    )
    grad, local, *backs = call(
        fine_inputs_kernel,
        [shaped((EDGE, D), bf16), stored((NODE, D), f32)] + [rim] * 4,
        (core, odd),
        (sender, receiver, edge_cotangent, edge_mixer, grad_act),
        (),
    )
    backs = to_partners(*backs)
    total, terms, *backs = lax.optimization_barrier((total, terms, *backs))
    (total,) = call(band_sum_kernel, [shaped((16, 16, D), bf16)], (), (), (terms, total))
    total = swapped_blocks(total, ("xhi", "z"))
    (near,) = call(
        rim_sum_kernel,
        [shaped((NODE, D), f32)],
        (core, odd, halo_send),
        (base, local),
        backs,
        [pltpu.VMEM((RIM, D), f32)],
    )
    node_grad, mix_part, out_part, node_mix_part, node_out_part = call(
        finish_kernel,
        [
            shaped((NODE, D), bf16),
            shaped((3, 2 * D), f32),
            shaped((1, 2 * D), f32),
            shaped((2, 2 * D), f32),
            shaped((1, 2 * D), f32),
        ],
        (coarse_row,),
        (),
        (total, near),
        [pltpu.VMEM((NODE, D), f32)],
    )
    return (
        node_update,
        update,
        cupdate,
        node_grad,
        grad,
        cgrad,
        mix_part,
        out_part.reshape(-1),
        node_mix_part,
        node_out_part.reshape(-1),
    )


def solution(mesh):
    fine = Mesh(np.asarray(mesh.devices).reshape(SHAPE), ALL)
    rows = P(ALL, None)
    flat = P(ALL)
    in_specs = (
        rows,
        rows,
        rows,
        flat,
        flat,
        P(ALL, None, None),
        flat,
        flat,
        flat,
        P(),
        P(),
        P(),
        P(),
        rows,
        rows,
        rows,
    )
    out_specs = (rows, rows, rows, rows, rows, rows, P(None, ALL), flat, P(None, ALL), flat)
    return jax.shard_map(shards, mesh=fine, in_specs=in_specs, out_specs=out_specs, check_vma=False)
```

```python
import jax
import jax.numpy as jnp
import numpy as np
from jax import lax
from jax.experimental import pallas as pl
from jax.experimental.pallas import tpu as pltpu
from jax.sharding import Mesh
from jax.sharding import PartitionSpec as P

epsilon = 1e-05
bf16 = jnp.bfloat16
f32 = jnp.float32

ALL = ("xhi", "z", "core", "xlo", "y")
SHAPE = (2, 8, 2, 2, 4)
LON = ("xhi", "z", "core")
LAT = ("xlo", "y")
CHIPS = ("xhi", "z", "xlo", "y")
D = 512
NODE = 32
EDGE = 256
CEDGE = 8
RIM = 8
PAIR = 2 * CEDGE
TABLE = NODE + 4 * RIM


def dot(left, right):
    return lax.dot_general(left, right, (((1,), (0,)), ((), ())), preferred_element_type=f32)


def dot_nt(left, right):
    return lax.dot_general(left, right, (((1,), (1,)), ((), ())), preferred_element_type=f32)


def dot_tn(left, right):
    return lax.dot_general(left, right, (((0,), (0,)), ((), ())), preferred_element_type=f32)


def sigmoid(v):
    return 1.0 / (1.0 + jnp.exp(-v))


def normalize(values):
    center = values - jnp.mean(values, -1, keepdims=True)
    spread = jnp.mean(center * center, -1, keepdims=True)
    scale_r = lax.rsqrt(spread + epsilon)
    return (center * scale_r, scale_r)


def normalize_back(normed, scale_r, incoming):
    mean_g = jnp.mean(incoming, -1, keepdims=True)
    mean_gy = jnp.mean(incoming * normed, -1, keepdims=True)
    return scale_r * (incoming - mean_g - normed * mean_gy)


def swish_slope(values):
    sigma = sigmoid(values)
    return sigma * (1.0 + values * (1.0 - sigma))


def pick_t(count, targets):
    shape = (count, targets.shape[1])
    hit = lax.broadcasted_iota(jnp.int32, shape, 0) == targets
    return jnp.where(hit, 1.0, 0.0).astype(bf16)


def order_matrix(core, first, count):
    wide = (count, 128)
    p = lax.broadcasted_iota(jnp.int32, wide, 0) + first
    side = lax.bitwise_xor(p >> 8, core)
    f = (((p >> 1) & 15) << 5) + (side << 4) + (((p >> 5) & 7) << 1) + (p & 1)
    lane = lax.broadcasted_iota(jnp.int32, wide, 1)
    parts = [jnp.where(f == lane + 128 * j, 1.0, 0.0).astype(bf16) for j in range(D // 128)]
    return jnp.concatenate(parts, axis=1)


def fold(row):
    return jnp.concatenate([row[:, 128 * j : 128 * (j + 1)] for j in range(4)], axis=0)


def unfold(block):
    return jnp.concatenate([block[j : j + 1, :] for j in range(4)], axis=1)


def chip_of(c):
    return (c >> 5) * 8 + ((c >> 1) & 7)


def side_of(c):
    return (c >> 4) & 1


def coarse_ends(lists):
    return [(lists[:, 2 * k : 2 * k + 1] * 32.0 + lists[:, 2 * k + 1 : 2 * k + 2]).astype(jnp.int32) for k in range(2)]


def coarse_pick(c, core):
    shape = (c.shape[0], D)
    place = lax.bitwise_xor(side_of(c), core) * 256 + chip_of(c) * 2 + (c & 1)
    return jnp.where(lax.broadcasted_iota(jnp.int32, shape, 1) == place, 1.0, 0.0).astype(bf16)


def coarse_rows(same, other, table):
    table[0:1024, :] = same.astype(f32).reshape(1024, 128)
    table[1024:2048, :] = other.astype(f32).reshape(1024, 128)
    return jnp.concatenate([table[pl.ds(j, 512, stride=4), :] for j in range(4)], axis=1).astype(bf16)


def partner_lists(core, odd):
    return (1 - core, core, 3 - odd, 2 + odd)


def chosen(flag, one, zero):
    flag = flag.astype(f32)
    return one * flag + zero * (1.0 - flag)


def gather_kernel(coarse_row_ref, nodes_ref, spread_ref, table):
    table[...] = nodes_ref[...].astype(f32)
    rows = [fold(table[pl.ds(coarse_row_ref[r], 1), :]) for r in range(2)]
    block = jnp.concatenate(rows, axis=0).astype(bf16)
    spread_ref[...] = jnp.broadcast_to(block[None], spread_ref.shape)


def start_kernel(
    core_ref,
    odd_ref,
    halo_ref,
    csend_ref,
    crecv_ref,
    nodes_ref,
    cedges_ref,
    ccot_ref,
    h0,
    h1,
    h2,
    h3,
    own_ref,
    table,
    picked,
    own,
):
    table[...] = nodes_ref[...].astype(f32)
    own[0:CEDGE, :] = cedges_ref[...].astype(f32)
    own[CEDGE : 2 * CEDGE, :] = ccot_ref[...].astype(f32)
    own[2 * CEDGE :, :] = jnp.zeros((2 * CEDGE, D), f32)
    lane = lax.broadcasted_iota(jnp.int32, (1, 128), 1)
    for e in range(CEDGE):
        row = jnp.zeros((1, 128), f32)
        for at, c in enumerate((csend_ref[e], crecv_ref[e])):
            row = jnp.where(lane == 2 * at, (c >> 5).astype(f32), row)
            row = jnp.where(lane == 2 * at + 1, (c & 31).astype(f32), row)
        own[2 * CEDGE + e : 2 * CEDGE + e + 1, 0:128] = row
    own_ref[...] = own[...].astype(bf16)
    for k, out in zip(partner_lists(core_ref[0], odd_ref[0]), (h0, h1, h2, h3)):
        for h in range(RIM):
            picked[h : h + 1, :] = table[pl.ds(halo_ref[0, k, h], 1), :]
        out[...] = picked[...].astype(bf16)


def edge_forward(send, recv, rows, mixer_ref, output_ref):
    pre = dot(send, mixer_ref[0]) + dot(recv, mixer_ref[1]) + dot(rows, mixer_ref[2])
    hidden = (pre * sigmoid(pre)).astype(bf16)
    normed, scale_r = normalize(dot(hidden, output_ref[...]))
    return pre, hidden, normed, scale_r


def fine_forward_kernel(
    ready,
    core_ref,
    odd_ref,
    nodes_ref,
    sender_ref,
    receiver_ref,
    edges_ref,
    mixer_ref,
    output_ref,
    h0,
    h1,
    h2,
    h3,
    same_ref,
    other_ref,
    update_ref,
    agg_ref,
    gathered_ref,
    send_ref,
    recv_ref,
    pre_ref,
    hidden_ref,
    normed_ref,
    scale_ref,
):
    nodes = nodes_ref[...]
    gathered_ref[0:1024, :] = same_ref[...].astype(f32).reshape(1024, 128).astype(bf16)
    gathered_ref[1024:2048, :] = other_ref[...].astype(f32).reshape(1024, 128).astype(bf16)
    core, odd = core_ref[0], odd_ref[0]
    a, b, c, d = [h[...].astype(f32) for h in (h0, h1, h2, h3)]
    rims = [chosen(core, a, b), chosen(core, b, a), chosen(odd, c, d), chosen(odd, d, c)]
    table = jnp.concatenate([nodes.astype(f32)] + rims, axis=0).astype(bf16)
    into_t = pick_t(NODE, receiver_ref[...])
    send = dot_tn(pick_t(TABLE, sender_ref[...]), table).astype(bf16)
    recv = dot_tn(into_t, nodes).astype(bf16)
    send_ref[...] = send
    recv_ref[...] = recv
    ready()
    edges = edges_ref[...]
    pre, hidden, normed, scale_r = edge_forward(send, recv, edges, mixer_ref, output_ref)
    pre_ref[...] = pre
    hidden_ref[...] = hidden
    normed_ref[...] = normed
    scale_ref[...] = jnp.broadcast_to(scale_r, scale_ref.shape)
    message = normed.astype(bf16)
    update_ref[...] = (edges.astype(f32) + message.astype(f32)).astype(bf16)
    agg_ref[...] = dot(into_t, message)


def coarse_forward_kernel(
    core_ref,
    mixer_ref,
    output_ref,
    pair_ref,
    same_ref,
    other_ref,
    cupdate_ref,
    sums_ref,
    table,
    total,
):
    core = core_ref[0]
    pair = pair_ref[...].astype(f32)
    rows, _, lists = (
        jnp.concatenate([pair[CEDGE * k : CEDGE * (k + 1)], pair[CEDGE * (k + 4) : CEDGE * (k + 5)]], axis=0) for k in range(3)
    )
    latents = coarse_rows(same_ref[...], other_ref[...], table)
    ends = coarse_ends(lists)
    send, recv = (dot(coarse_pick(c, core), latents).astype(bf16) for c in ends)
    _, _, normed, _ = edge_forward(send, recv, rows.astype(bf16), mixer_ref, output_ref)
    message = normed.astype(bf16)
    cupdate_ref[...] = (rows + message.astype(f32))[0:CEDGE].astype(bf16)
    into = dot_tn(coarse_pick(ends[1], core), message)[0 : D // 2]
    for j in range(4):
        total[pl.ds(j, D // 2, stride=4), :] = into[:, 128 * j : 128 * (j + 1)]
    sums_ref[...] = total[...].reshape(128, 8, 128).astype(bf16)


def put_halves(keep_ref, give_ref, slot, grad):
    keep_ref[:, slot] = grad[0 : D // 2].astype(bf16).reshape(8, 32, D)
    give_ref[:, slot] = grad[D // 2 : D].astype(bf16).reshape(8, 32, D)


def node_kernel(
    coarse_row_ref,
    nodes_ref,
    mixer_ref,
    output_ref,
    cot_ref,
    sums_ref,
    agg_ref,
    update_ref,
    rounded_ref,
    hidden_ref,
    grad_update_ref,
    grad_pre_ref,
    grad_agg_ref,
    spread_ref,
):
    owned = jnp.sum(sums_ref[...].astype(f32), axis=0)
    place = lax.broadcasted_iota(jnp.int32, (NODE, D), 0)
    aggregate = agg_ref[...]
    for r in range(2):
        row = unfold(owned[4 * r : 4 * r + 4])
        aggregate = aggregate + jnp.where(place == coarse_row_ref[r], row, 0.0)
    rounded = aggregate.astype(bf16)
    rounded_ref[...] = rounded
    nodes = nodes_ref[...]
    cot = cot_ref[...].astype(f32)
    pre = dot(nodes, mixer_ref[0]) + dot(rounded, mixer_ref[1])
    hidden = (pre * sigmoid(pre)).astype(bf16)
    hidden_ref[...] = hidden
    normed, scale_r = normalize(dot(hidden, output_ref[...]))
    update_ref[...] = (nodes.astype(f32) + normed).astype(bf16)
    grad_update = normalize_back(normed, scale_r, cot).astype(bf16)
    grad_update_ref[...] = grad_update
    grad_pre = (dot_nt(grad_update, output_ref[...]) * swish_slope(pre)).astype(bf16)
    grad_pre_ref[...] = grad_pre
    grad_agg = dot_nt(grad_pre, mixer_ref[1]).astype(bf16)
    grad_agg_ref[...] = grad_agg
    wide = grad_agg.astype(f32)
    rows = []
    for r in range(2):
        row = jnp.sum(jnp.where(place == coarse_row_ref[r], wide, 0.0), axis=0, keepdims=True)
        rows.append(fold(row))
    block = jnp.concatenate(rows, axis=0).astype(bf16)
    spread_ref[...] = jnp.broadcast_to(block[None], spread_ref.shape)


def node_weights_kernel(
    core_ref, nodes_ref, cot_ref, mixer_ref, rounded_ref, hidden_ref, grad_update_ref, grad_pre_ref, base_ref, keep_ref, give_ref
):
    grad_pre = grad_pre_ref[...]
    base_ref[...] = cot_ref[...].astype(f32) + dot_nt(grad_pre, mixer_ref[0])
    order = order_matrix(core_ref[0], 0, D)
    for slot, (left, right) in enumerate(
        ((nodes_ref, grad_pre), (rounded_ref, grad_pre), (hidden_ref, grad_update_ref[...]))
    ):
        put_halves(keep_ref, give_ref, slot, dot(dot_nt(order, left[...]).astype(bf16), right))


def fine_backward_kernel(
    ready,
    core_ref,
    receiver_ref,
    cot_ref,
    pre_ref,
    normed_ref,
    scale_ref,
    output_ref,
    edges_ref,
    send_ref,
    recv_ref,
    hidden_ref,
    grad_agg_ref,
    grad_act_ref,
    keep_ref,
    give_ref,
):
    into_t = pick_t(NODE, receiver_ref[...])
    incoming = dot_tn(into_t, grad_agg_ref[...]) + cot_ref[...].astype(f32)
    grad_pre = normalize_back(normed_ref[...], scale_ref[:, 0:1], incoming).astype(bf16)
    grad_act = (dot_nt(grad_pre, output_ref[...]) * swish_slope(pre_ref[...])).astype(bf16)
    grad_act_ref[...] = grad_act
    order = order_matrix(core_ref[0], 0, D)
    ready()
    for slot, (left, right) in enumerate(
        ((send_ref, grad_act), (recv_ref, grad_act), (edges_ref, grad_act), (hidden_ref, grad_pre))
    ):
        put_halves(keep_ref, give_ref, slot, dot(dot_nt(order, left[...]).astype(bf16), right))


def fine_inputs_kernel(
    core_ref, odd_ref, sender_ref, receiver_ref, cot_ref, mixer_ref, grad_act_ref, grad_ref, local_ref, g0, g1, g2, g3
):
    into_t = pick_t(NODE, receiver_ref[...])
    from_t = pick_t(TABLE, sender_ref[...])
    grad_act = grad_act_ref[...]
    to_sender = dot_nt(dot(from_t, grad_act).astype(bf16), mixer_ref[0])
    to_receiver = dot_nt(dot(into_t, grad_act).astype(bf16), mixer_ref[1])
    local_ref[...] = to_sender[0:NODE] + to_receiver
    core, odd = core_ref[0], odd_ref[0]
    a, b, c, d = [to_sender[NODE + RIM * k : NODE + RIM * (k + 1)] for k in range(4)]
    rims = [chosen(core, a, b), chosen(core, b, a), chosen(odd, c, d), chosen(odd, d, c)]
    for rim, out in zip(rims, (g0, g1, g2, g3)):
        out[...] = rim.astype(bf16)
    grad_ref[...] = (cot_ref[...].astype(f32) + dot_nt(grad_act, mixer_ref[2])).astype(bf16)


def chip_sum_kernel(keep_n, keep_f, got_f, got_n, out_ref):
    for d in range(8):
        out_ref[d, 0:4] = (keep_f[d].astype(f32) + got_f[d].astype(f32)).astype(bf16)
        out_ref[d, 4:7] = (keep_n[d].astype(f32) + got_n[d].astype(f32)).astype(bf16)


def coarse_backward_kernel(
    core_ref,
    band_ref,
    gathered_ref,
    mixer_ref,
    output_ref,
    near_edges_ref,
    far_edges_ref,
    same_ref,
    other_ref,
    cgrad_ref,
    terms_ref,
    table,
):
    core, band = core_ref[0], band_ref[0]

    count = 8 * PAIR
    wide = jnp.concatenate([near_edges_ref[...].astype(f32), far_edges_ref[...].astype(f32)], axis=0)
    wide = wide.reshape(8, 2, 4 * CEDGE, D)
    rows, cot, lists = (
        wide[:, :, CEDGE * k : CEDGE * (k + 1)].reshape(count, D) for k in range(3)
    )
    ends = coarse_ends(lists)

    def pick_owned(c):
        mine = (side_of(c) == core) & (((c >> 1) & 7) == band)
        place = jnp.where(mine, (c >> 5) * 2 + (c & 1), -1)
        hit = lax.broadcasted_iota(jnp.int32, (count, 128), 1) == place
        return jnp.where(hit, 1.0, 0.0).astype(bf16)

    rows = rows.astype(bf16)
    latents = coarse_rows(gathered_ref[0:1024, :], gathered_ref[1024:2048, :], table)
    send = dot(coarse_pick(ends[0], core), latents).astype(bf16)
    into = coarse_pick(ends[1], core)
    recv = dot(into, latents).astype(bf16)
    pre, hidden, normed, scale_r = edge_forward(send, recv, rows, mixer_ref, output_ref)
    incoming = dot(into, coarse_rows(same_ref[...], other_ref[...], table)) + cot
    grad_pre = normalize_back(normed, scale_r, incoming).astype(bf16)
    grad_act = (dot_nt(grad_pre, output_ref[...]) * swish_slope(pre)).astype(bf16)
    cgrad_ref[...] = (cot[0:PAIR] + dot_nt(grad_act[0:PAIR], mixer_ref[2]))[0:CEDGE].astype(bf16)

    owned = 2 * 16
    by_sender = dot_tn(pick_owned(ends[0]), grad_act)[0:owned].astype(bf16)
    by_receiver = dot_tn(pick_owned(ends[1]), grad_act)[0:owned].astype(bf16)
    terms_ref[4] = dot_nt(by_sender, mixer_ref[0]) + dot_nt(by_receiver, mixer_ref[1])
    p = lax.broadcasted_iota(jnp.int32, (owned, D), 0)
    f = ((p >> 1) << 5) + (core << 4) + (band << 1) + (p & 1)
    order = jnp.where(f == lax.broadcasted_iota(jnp.int32, (owned, D), 1), 1.0, 0.0).astype(bf16)
    for slot, (left, right) in enumerate(((send, grad_act), (recv, grad_act), (rows, grad_act), (hidden, grad_pre))):
        terms_ref[slot] = dot(dot_nt(order, left).astype(bf16), right)


def band_sum_kernel(terms_ref, in_ref, out_ref):
    total = in_ref[0].astype(f32)
    for d in range(1, 8):
        total = total + in_ref[d].astype(f32)
    terms = terms_ref[...]
    total = jnp.concatenate([total[0:4] + terms[0:4], terms[4:5], total[4:7]], axis=0)
    total = total.reshape(256, D).astype(bf16)
    place = lax.broadcasted_iota(jnp.int32, (256, 256), 0)
    source = ((place >> 1) & 7) * 32 + (place >> 4) * 2 + (place & 1)
    hit = source == lax.broadcasted_iota(jnp.int32, (256, 256), 1)
    ordered = dot(jnp.where(hit, 1.0, 0.0).astype(bf16), total).astype(bf16)
    out_ref[...] = ordered.reshape(16, 16, D)


def rim_sum_kernel(core_ref, odd_ref, halo_ref, base_ref, local_ref, r0, r1, r2, r3, near_ref, back):
    near_ref[...] = base_ref[...] + local_ref[...]
    for k, got in zip(partner_lists(core_ref[0], odd_ref[0]), (r0, r1, r2, r3)):
        back[...] = got[...].astype(f32)
        for h in range(RIM):
            at = pl.ds(halo_ref[0, k, h], 1)
            near_ref[at, :] = near_ref[at, :] + back[h : h + 1, :]


def finish_kernel(
    coarse_row_ref,
    sums_ref,
    near_ref,
    node_grad_ref,
    mix_ref,
    out_ref,
    node_mix_ref,
    node_out_ref,
    total,
):
    owned = jnp.sum(sums_ref[...].astype(f32), axis=0)
    total[...] = near_ref[...]
    for r in range(2):
        at = pl.ds(coarse_row_ref[r], 1)
        total[at, :] = total[at, :] + owned[8 + r : 9 + r]
        wide = slice(D * r, D * (r + 1))
        for a in range(3):
            mix_ref[a : a + 1, wide] = owned[2 * a + r : 2 * a + r + 1]
        out_ref[:, wide] = owned[6 + r : 7 + r]
        for a in range(2):
            node_mix_ref[a : a + 1, wide] = owned[10 + 2 * a + r : 11 + 2 * a + r]
        node_out_ref[:, wide] = owned[14 + r : 15 + r]
    node_grad_ref[...] = total[...].astype(bf16)


def call(kernel, outs, scalars, far, near, scratch=(), us=1, late=0):
    hbm = pl.BlockSpec(memory_space=pltpu.HBM)

    def space(x):
        return pl.BlockSpec(memory_space=pltpu.SMEM if x.dtype == jnp.int32 else pltpu.VMEM)

    fetched = [pltpu.with_memory_space_constraint(x, pltpu.HBM) for x in (*scalars, *far)]
    held = [pltpu.SMEM(x.shape, x.dtype) for x in scalars] + [pltpu.VMEM(x.shape, x.dtype) for x in far]
    count = len(fetched)

    def body(*refs):
        sources, refs = refs[:count], refs[count:]
        passed, refs = refs[: len(near) + len(outs)], refs[len(near) + len(outs) :]
        slots, sems, rest = refs[:count], refs[count], refs[count + 1 :]
        copies = [pltpu.make_async_copy(x, y, sems.at[i]) for i, (x, y) in enumerate(zip(sources, slots))]
        for copy in copies:
            copy.start()
        for copy in copies[: count - late]:
            copy.wait()

        def ready():
            for copy in copies[count - late :]:
                copy.wait()

        kernel(*([ready] if late else []), *slots, *passed, *rest)

    moved = sum(int(np.prod(x.shape)) * x.dtype.itemsize for x in (*fetched, *near, *outs))
    return pl.pallas_call(
        body,
        out_shape=outs,
        in_specs=[hbm] * count + [space(x) for x in near],
        out_specs=[space(x) for x in outs],
        scratch_shapes=[*held, pltpu.SemaphoreType.DMA((max(count, 1),)), *scratch],
        compiler_params=pltpu.CompilerParams(vmem_limit_bytes=24 * 2**20),
        cost_estimate=pl.CostEstimate(flops=us * 1_150_000_000, bytes_accessed=moved, transcendentals=0),
    )(*fetched, *near)


def shaped(shape, dtype):
    return jax.ShapeDtypeStruct(shape, dtype)


def stored(shape, dtype):
    return pltpu.HBM(shape, dtype)


def swap(x):
    return lax.ppermute(x, "core", [(0, 1), (1, 0)])


def to_partners(a, b, c, d):
    def exchange(x, axes, pairs):
        return lax.ppermute(x, axes, pairs + [(j, i) for i, j in pairs])

    a = swap(a)
    c = exchange(c, LAT, [(i, i + 1) for i in range(0, 8, 2)])
    d = exchange(d, LAT, [(i, i + 1) for i in range(1, 7, 2)])
    b = exchange(b, LON, [(i, (i + 1) % 32) for i in range(1, 32, 2)])
    return (a, b, c, d)


def across(x, mask):
    return lax.ppermute(x, LAT, [(i, i ^ mask) for i in range(8)])


def doubled(x, mask):
    return jnp.concatenate([x, across(x, mask)], axis=0)


def swapped_blocks(x, axes):
    return lax.all_to_all(x, axes, 0, 0, tiled=True)


def shards(
    node_latents,
    edge_latents,
    coarse_edges,
    sender,
    receiver,
    halo_send,
    coarse_row,
    coarse_sender,
    coarse_receiver,
    edge_mixer,
    edge_output,
    node_mixer,
    node_output,
    node_cotangent,
    edge_cotangent,
    coarse_cotangent,
):
    core = lax.axis_index("core").astype(jnp.int32).reshape(1)
    odd = (lax.axis_index("y") & 1).astype(jnp.int32).reshape(1)
    band = lax.axis_index(LAT).astype(jnp.int32).reshape(1)
    sender = sender.reshape(1, EDGE)
    receiver = receiver.reshape(1, EDGE)
    rim = shaped((RIM, D), bf16)
    blocks = shaped((128, 8, 128), bf16)

    def kept(count):
        return [
            stored((count, D), bf16),
            stored((count, D), bf16),
            stored((count, D), f32),
            stored((count, D), bf16),
            stored((count, D), f32),
            stored((count, 128), f32),
        ]

    (spread,) = call(gather_kernel, [blocks], (coarse_row,), (node_latents,), (), [pltpu.VMEM((NODE, D), f32)])
    *rims, own = call(
        start_kernel,
        [rim] * 4 + [shaped((4 * CEDGE, D), bf16)],
        (core, odd, halo_send, coarse_sender, coarse_receiver),
        (node_latents,),
        (coarse_edges, coarse_cotangent),
        [pltpu.VMEM((NODE, D), f32), pltpu.VMEM((RIM, D), f32), pltpu.VMEM((4 * CEDGE, D), f32)],
    )
    same = swapped_blocks(spread, CHIPS)
    pair = jnp.concatenate([own, swap(own)], axis=0)
    rims = to_partners(*rims)
    same, pair, *rims = lax.optimization_barrier((same, pair, *rims))
    other = swap(same)
    cupdate, sums = call(
        coarse_forward_kernel,
        [shaped((CEDGE, D), bf16), blocks],
        (core,),
        (),
        (edge_mixer, edge_output, pair, same, other),
        [pltpu.VMEM((2048, 128), f32), pltpu.VMEM((1024, 128), f32)],
        us=3,
    )
    sums, pair, *rims = lax.optimization_barrier((sums, pair, *rims))
    sums = swapped_blocks(sums, CHIPS)
    known = doubled(doubled(pair, 1), 2)
    update, agg, gathered, *fine = call(
        fine_forward_kernel,
        [shaped((EDGE, D), bf16), shaped((NODE, D), f32), stored((2048, 128), bf16)] + kept(EDGE),
        (core, odd),
        (node_latents, sender, receiver, edge_latents, edge_mixer, edge_output),
        (*rims, same, other),
        us=4,
        late=3,
    )
    sums, known, agg = lax.optimization_barrier((sums, known, agg))
    small = shaped((NODE, D), bf16)
    node_update, *node_kept, grad_agg, spread = call(
        node_kernel,
        [small] + [stored((NODE, D), bf16)] * 4 + [small, blocks],
        (coarse_row,),
        (),
        (node_latents, node_mixer, node_output, node_cotangent, sums, agg),
        us=3,
    )
    spread, known, grad_agg = lax.optimization_barrier((spread, known, grad_agg))
    same = swapped_blocks(spread, CHIPS)
    far_half = across(known, 4)
    base, keep_n, give_n = call(
        node_weights_kernel,
        [stored((NODE, D), f32)] + [shaped((8, 3, 32, D), bf16)] * 2,
        (core,),
        (node_latents, node_cotangent, node_mixer, *node_kept),
        (),
        us=3,
    )
    send_rows, recv_rows, pre, hidden, normed, scale_r = fine
    grad_act, keep_f, give_f = call(
        fine_backward_kernel,
        [stored((EDGE, D), bf16)] + [shaped((8, 4, 32, D), bf16)] * 2,
        (core,),
        (receiver, edge_cotangent, pre, normed, scale_r, edge_output, edge_latents, send_rows, recv_rows, hidden),
        (grad_agg,),
        us=5,
        late=4,
    )
    same, keep_f, give_f, keep_n, give_n, far_half = lax.optimization_barrier(
        (same, keep_f, give_f, keep_n, give_n, far_half)
    )
    (total,) = call(
        chip_sum_kernel,
        [shaped((8, 7, 32, D), bf16)],
        (),
        (),
        (keep_n, keep_f, swap(give_f), swap(give_n)),
    )
    total, same, grad_act = lax.optimization_barrier((total, same, grad_act))
    total = swapped_blocks(total, LAT)
    other = swap(same)
    cgrad, terms = call(
        coarse_backward_kernel,
        [shaped((CEDGE, D), bf16), shaped((5, 32, D), f32)],
        (core, band),
        (gathered, edge_mixer, edge_output),
        (known, far_half, same, other),
        [pltpu.VMEM((2048, 128), f32)],
    )
    grad, local, *backs = call(
        fine_inputs_kernel,
        [shaped((EDGE, D), bf16), stored((NODE, D), f32)] + [rim] * 4,
        (core, odd),
        (sender, receiver, edge_cotangent, edge_mixer, grad_act),
        (),
    )
    backs = to_partners(*backs)
    total, terms, *backs = lax.optimization_barrier((total, terms, *backs))
    (total,) = call(band_sum_kernel, [shaped((16, 16, D), bf16)], (), (), (terms, total))
    total = swapped_blocks(total, ("xhi", "z"))
    (near,) = call(
        rim_sum_kernel,
        [shaped((NODE, D), f32)],
        (core, odd, halo_send),
        (base, local),
        backs,
        [pltpu.VMEM((RIM, D), f32)],
    )
    node_grad, mix_part, out_part, node_mix_part, node_out_part = call(
        finish_kernel,
        [
            shaped((NODE, D), bf16),
            shaped((3, 2 * D), f32),
            shaped((1, 2 * D), f32),
            shaped((2, 2 * D), f32),
            shaped((1, 2 * D), f32),
        ],
        (coarse_row,),
        (),
        (total, near),
        [pltpu.VMEM((NODE, D), f32)],
    )
    return (
        node_update,
        update,
        cupdate,
        node_grad,
        grad,
        cgrad,
        mix_part,
        out_part.reshape(-1),
        node_mix_part,
        node_out_part.reshape(-1),
    )


def solution(mesh):
    fine = Mesh(np.asarray(mesh.devices).reshape(SHAPE), ALL)
    rows = P(ALL, None)
    flat = P(ALL)
    in_specs = (
        rows,
        rows,
        rows,
        flat,
        flat,
        P(ALL, None, None),
        flat,
        flat,
        flat,
        P(),
        P(),
        P(),
        P(),
        rows,
        rows,
        rows,
    )
    out_specs = (rows, rows, rows, rows, rows, rows, P(None, ALL), flat, P(None, ALL), flat)
    return jax.shard_map(shards, mesh=fine, in_specs=in_specs, out_specs=out_specs, check_vma=False)
```
